256 devices in a mesh: grp: 8 (over x, y_lo), head: 32 (over y_hi, z, core).
Axes of the slice: x: 4, y: 4 (y_hi: 2, y_lo: 2; y = y_hi * 2 + y_lo), z: 8, core: 2. Of those that a mesh axis runs over, the one named last changes fastest.
Arguments:
- kv_pool: bfloat16 [2, 352, 128, 12288], P(None, 'grp', None, 'head'), may hold values from -6 to 6
- qkv_new: bfloat16 [3, 4, 256, 12288], P(None, None, 'grp', 'head'), may hold values from -119 to 119
- w_out: bfloat16 [12288, 6144], P('head'), may hold values from -0.109375 to 0.109375
- table: int32 [256, 4], P('grp'), may hold values from 0 to 43, as said below
- lengths: int32 [256], replicated, may hold values from 0 to 512, as said below
- migration: int32 [16, 2], replicated, may hold values from 0 to 30, as said below
Outputs:
- mixed: bfloat16 [4, 256, 6144], P(None, 'grp', 'head')
The draws below stay inside these ranges and needn't reach their ends.
Inputs may be any that keep to these rules, and one draw needn't show every extreme that they name: `table`: within a group, the pages of resident slots' first ceil(length / 128) entries are distinct numbers below 36; later entries repeat the last used page; landing slots' rows are 36 + m * 4 + j. Landing slots have length 0. In each pair of partner groups exactly one moves out 2 of its resident requests, whose lengths exceed (3) * 128; all other resident lengths are at most 128. `migration`: rows of a group that moves: distinct resident slots and arrivals in 0 to 3; rows of the other group: slot 30 and arrival 0.
All inputs are finite; a program needn't handle non-finite values.
Results may differ from the reference program's by a relative error of at most 0.02.
Values may be sent and summed in bfloat16 or wider, within the bound.
A program may use at most 128 MiB of HBM per device.

```python
import jax
import jax.numpy as jnp
from jax import lax

STEPS = 4
LIVE = 30
MOVES = 2
SLOTS = 32
MAXP = 4
PAGE = 128
LIVE_PAGES = 36
PAGES = 44
HEADS = 96
HD = 128
D_OUT = 6144
N_GRP = 8


def plan_draw(key):
    half = N_GRP // 2
    key_side, key_order, key_long, key_short, key_arr, key_pages = jax.random.split(key, 6)
    side = jax.random.randint(key_side, (half,), 0, 2).astype(jnp.int32)
    groups = jnp.arange(N_GRP, dtype=jnp.int32)
    busy = groups // half == side[groups % half]
    live_ids = jnp.arange(LIVE, dtype=jnp.int32)
    order_score = jax.random.randint(key_order, (N_GRP, LIVE), 0, 1 << 20) * LIVE + live_ids[None, :]
    slot_order = jnp.argsort(order_score, axis=1).astype(jnp.int32)
    moved_slots = slot_order[:, :MOVES]
    is_moved = jnp.any(live_ids[None, :, None] == moved_slots[:, None, :], -1) & busy[:, None]
    long_len = jax.random.randint(key_long, (N_GRP, LIVE), (MAXP - 1) * PAGE + 1, MAXP * PAGE + 1)
    short_len = jax.random.randint(key_short, (N_GRP, LIVE), 1, PAGE + 1)
    live_len = jnp.where(is_moved, long_len, short_len).astype(jnp.int32)
    first_busy = side[0] * half
    forced = (groups[:, None] == first_busy) & (live_ids[None, :] == moved_slots[:, :1])
    live_len = jnp.where(forced, MAXP * PAGE, live_len).astype(jnp.int32)
    all_len = jnp.concatenate([live_len, jnp.zeros((N_GRP, MOVES), jnp.int32)], 1)
    move_ids = jnp.arange(MOVES, dtype=jnp.int32)
    arrival = jax.random.randint(key_arr, (N_GRP, MOVES), 0, STEPS).astype(jnp.int32)
    fixed_arr = jnp.where(move_ids == 0, 0, STEPS - 1).astype(jnp.int32)
    arrival = jnp.where(groups[:, None] == first_busy, fixed_arr[None, :], arrival)
    plan_slot = jnp.where(busy[:, None], moved_slots, LIVE)
    plan_arr = jnp.where(busy[:, None], arrival, 0)
    all_plan = jnp.stack([plan_slot, plan_arr], -1).astype(jnp.int32)
    page_need = (live_len + PAGE - 1) // PAGE
    offset = jnp.cumsum(page_need, axis=1) - page_need
    page_score = jax.random.randint(key_pages, (N_GRP, LIVE_PAGES), 0, 1 << 20) * LIVE_PAGES
    page_score = page_score + jnp.arange(LIVE_PAGES, dtype=jnp.int32)[None, :]
    page_perm = jnp.argsort(page_score, axis=1).astype(jnp.int32)
    page_slot = jnp.arange(MAXP, dtype=jnp.int32)
    position = offset[:, :, None] + jnp.minimum(page_slot[None, None, :], page_need[:, :, None] - 1)
    live_table = jnp.take_along_axis(page_perm, position.reshape(N_GRP, LIVE * MAXP), axis=1)
    live_table = live_table.reshape(N_GRP, LIVE, MAXP)
    land_table = LIVE_PAGES + move_ids[:, None] * MAXP + page_slot[None, :]
    land_table = jnp.broadcast_to(land_table[None], (N_GRP, MOVES, MAXP))
    all_table = jnp.concatenate([live_table, land_table], 1).astype(jnp.int32)
    return (all_table.reshape(N_GRP * SLOTS, MAXP), all_len.reshape(N_GRP * SLOTS), all_plan.reshape(N_GRP * MOVES, 2))


def draw_table(key, part):
    base_key = key
    return plan_draw(base_key)[0]


def draw_lengths(key, part):
    base_key = key
    return plan_draw(base_key)[1]


def draw_migration(key, part):
    base_key = key
    return plan_draw(base_key)[2]


def draw_qkv_new(key, part):
    key = jax.random.fold_in(key, 7)
    key_vals = jax.random.fold_in(key, 0)
    shape = (3, STEPS, N_GRP * SLOTS, HEADS * HD)
    values = jnp.clip(jax.random.normal(key_vals, shape, jnp.float32), -5.0, 5.0)
    return values.astype(jnp.bfloat16)


def spiked(values, key, source, target, blocks, factor):
    def block_of(axis_at):
        return (jnp.arange(values.shape[axis_at]) // (values.shape[axis_at] // blocks)).reshape((-1,) + (1,) * (values.ndim - 1 - axis_at))

    first = jax.random.permutation(key, blocks)[block_of(target)]
    second = (block_of(target) + blocks // 2) % blocks
    return jnp.where((block_of(source) == first) | (block_of(source) == second), factor * values, values)


def level_of(own_key, shape, shards, low, high):
    def one(axis_at, blocks):
        draws = jax.random.uniform(jax.random.fold_in(jax.random.fold_in(own_key, 6), axis_at), (blocks,), jnp.float32, low / len(shards), high / len(shards))
        return jnp.repeat(jnp.exp(draws), shape[axis_at] // blocks).reshape((-1,) + (1,) * (len(shape) - axis_at - 1))

    level = one(*shards[0])
    for cut in shards[1:]:
        level = level * one(*cut)
    return level


def bell_draw(key, dims, deviation, bound, shards=(), held_as=jnp.bfloat16):
    values = jax.random.normal(key, dims, jnp.float32) * deviation
    if len(shards) > 0:
        values = level_of(key, dims, shards, -0.22, 0.18) * values
    return jnp.clip(values, min=-bound, max=bound).astype(held_as)


def noise_with(rng, dims, deviation, most, pieces, heavy, held_as=jnp.bfloat16):
    entries = deviation * jax.random.normal(rng, dims, jnp.float32)
    if pieces:
        entries = entries * level_of(rng, dims, pieces, -0.22, 0.18)
    return jnp.clip(spiked(entries, jax.random.fold_in(rng, 3), *heavy), -most, most).astype(held_as)


def setup_inputs(seed: int = 0) -> dict:
    key_of = jax.random.split(jax.random.key(seed), 7)
    kv_pool = bell_draw(key_of[0], (2, N_GRP * PAGES, PAGE, HEADS * HD), 1.0, 6.0, ((1, 8), (3, 32)))
    qkv_new = draw_qkv_new(jax.random.fold_in(key_of[6], 71), 0)
    w_out = noise_with(key_of[2], (HEADS * HD, D_OUT), (HEADS * HD) ** -0.5, 0.109375, ((0, 32),), (0, 1, 32, 2.75))
    table = draw_table(jax.random.fold_in(key_of[6], 71), 0)
    lengths = draw_lengths(jax.random.fold_in(key_of[6], 71), 0)
    migration = draw_migration(jax.random.fold_in(key_of[6], 71), 0)
    return {"kv_pool": kv_pool, "qkv_new": qkv_new, "w_out": w_out, "table": table, "lengths": lengths, "migration": migration}


def attend_one(queries, cache_keys, cache_vals, key_valid, new_keys, new_vals):
    scale = HD ** -0.5
    query_f = queries.astype(jnp.float32)
    cache_score = jnp.einsum("shd,khd->hsk", query_f, cache_keys.astype(jnp.float32)) * scale
    cache_score = jnp.where(key_valid[None, None, :], cache_score, -jnp.inf)
    new_score = jnp.einsum("shd,uhd->hsu", query_f, new_keys.astype(jnp.float32)) * scale
    step_ids = jnp.arange(queries.shape[0], dtype=jnp.int32)
    causal = step_ids[:, None] >= step_ids[None, :]
    new_score = jnp.where(causal[None], new_score, -jnp.inf)
    top_score = jnp.maximum(jnp.max(cache_score, -1), jnp.max(new_score, -1))
    cache_exp = jnp.exp(cache_score - top_score[..., None])
    new_exp = jnp.exp(new_score - top_score[..., None])
    total = jnp.sum(cache_exp, -1) + jnp.sum(new_exp, -1)
    cache_wts = (cache_exp / total[..., None]).astype(jnp.bfloat16)
    new_wts = (new_exp / total[..., None]).astype(jnp.bfloat16)
    mixed_out = jnp.einsum("hsk,khd->shd", cache_wts.astype(jnp.float32), cache_vals.astype(jnp.float32))
    mixed_out = mixed_out + jnp.einsum("hsu,uhd->shd", new_wts.astype(jnp.float32), new_vals.astype(jnp.float32))
    return mixed_out.astype(jnp.bfloat16)


def reference(kv_pool, qkv_new, w_out, table, lengths, migration):
    feat_width = HEADS * HD
    all_plan = migration.reshape(N_GRP, MOVES, 2)
    all_len = lengths.reshape(N_GRP, SLOTS)
    all_table = table.reshape(N_GRP, SLOTS, MAXP)
    new_all = qkv_new.reshape(3, STEPS, N_GRP, SLOTS, feat_width)
    step_ids = jnp.arange(STEPS, dtype=jnp.int32)

    def one_slot(location):
        grp_index = location // SLOTS
        slot_index = location % SLOTS
        partner = jnp.bitwise_xor(grp_index, N_GRP // 2)
        landing = slot_index >= LIVE
        move_index = jnp.clip(slot_index - LIVE, 0, MOVES - 1)
        part_slot = all_plan[partner, move_index, 0]
        part_arr = all_plan[partner, move_index, 1]
        leave_step = jnp.min(jnp.where(all_plan[grp_index, :, 0] == slot_index, all_plan[grp_index, :, 1], STEPS))
        src_group = jnp.where(landing, partner, grp_index)
        src_slot = jnp.where(landing, part_slot, slot_index)
        src_len = all_len[src_group, src_slot]
        served = jnp.where(landing, (part_slot < LIVE) & (step_ids >= part_arr), step_ids < leave_step)
        arrival = jnp.where(landing, part_arr, 0)
        own_new = new_all[:, :, grp_index, slot_index]
        src_new = new_all[:, :, src_group, src_slot]
        history = jnp.where((step_ids < arrival)[None, :, None], src_new[1:], own_new[1:])
        page_ids = (src_group * PAGES + all_table[src_group, src_slot]).astype(jnp.int32)
        cache = kv_pool[:, page_ids].reshape(2, MAXP * PAGE, HEADS, HD)
        key_valid = jnp.arange(MAXP * PAGE, dtype=jnp.int32) < src_len
        result = attend_one(own_new[0].reshape(STEPS, HEADS, HD), cache[0], cache[1], key_valid,
                            history[0].reshape(STEPS, HEADS, HD), history[1].reshape(STEPS, HEADS, HD))
        result = result.reshape(STEPS, feat_width)
        return jnp.where(served[:, None], result, jnp.zeros_like(result))

    attn = lax.map(one_slot, jnp.arange(N_GRP * SLOTS, dtype=jnp.int32))
    attn_rows = jnp.transpose(attn, (1, 0, 2)).reshape(STEPS * N_GRP * SLOTS, feat_width)
    mixed = jnp.dot(attn_rows, w_out, preferred_element_type=jnp.float32).astype(jnp.bfloat16)
    return mixed.reshape(STEPS, N_GRP * SLOTS, D_OUT)
```

```python
import jax
import jax.numpy as jnp
from jax import lax
from jax.experimental import pallas as pl
from jax.experimental.pallas import tpu as pltpu
from jax.sharding import PartitionSpec as P

MESH = pl.DeviceIdType.MESH
HD = 128
HEADS = 3
FEAT = HEADS * HD
STEPS = 4
SLOTS = 32
LIVE = 30
LIVE_PAGES = 36
PAGE = 128
MAXP = 4
ROWS = STEPS * SLOTS
RPS = 16
CHUNKS = 4
NZ = 8
Z_ORDER = (4, 3, 5, 2, 6, 1, 7, 0)
UNIT = 192
F32 = jnp.float32
BF16 = jnp.bfloat16
SCALE = HD ** -0.5


def iota(shape, dim):
    return lax.broadcasted_iota(jnp.int32, shape, dim)


def one_hot(cond):
    return jnp.where(cond, 1.0, 0.0).astype(BF16)


def dot(a, b):
    return jnp.dot(a, b, preferred_element_type=F32)


def dot_t(a, b):
    return lax.dot_general(a, b, (((1,), (1,)), ((), ())), preferred_element_type=F32)


def kernel(kv, qkv, w, table, lens, plan, out,
           kbuf, vbuf, wbuf, ext, land_src, land_dst, moved_src, moved_dst,
           qb, sc, sn, scm, snm, pc, pn, on, ob, attn,
           own, core_src, core_dst, y_src, y_dst, z_src, z_dst,
           k_sem, v_sem, w_sem, q_sem, land_sem, moved_sem, core_ssem, core_rsem, y_ssem, y_rsem, z_ssem, z_rsem):
    g = lax.axis_index("grp")
    h = lax.axis_index("head")
    yh, z, core = h // 16, lax.rem(h // 2, NZ), lax.rem(h, 2)
    sibling = (g, h + 1 - 2 * core)
    y_peer = (g, lax.rem(h + 16, 32))
    x_peer = (lax.rem(g + 4, 8), h)

    def z_peer(d):
        return (g, yh * 16 + lax.rem(z + d, NZ) * 2 + core)

    q_copy = pltpu.make_async_copy(qkv, ext.at[:, pl.ds(0, ROWS)], q_sem)
    q_copy.start()
    per = LIVE_PAGES // CHUNKS

    def page_copies(which, buf, sem):
        return [pltpu.make_async_copy(kv.at[which, pl.ds(n * per, per)], buf.at[pl.ds(n * per, per)], sem.at[n])
                for n in range(CHUNKS)]

    k_copies = page_copies(0, kbuf, k_sem)
    v_copies = page_copies(1, vbuf, v_sem)
    for cp in k_copies + v_copies:
        cp.start()

    barrier = pltpu.get_barrier_semaphore()
    peers = [sibling, y_peer, x_peer] + [z_peer(d) for d in range(1, NZ)]
    for peer in peers:
        pl.semaphore_signal(barrier, inc=1, device_id=peer, device_id_type=MESH)

    def w_copies(k):
        u, d = k // NZ, Z_ORDER[k % NZ]
        b = (1 - yh) if u == 0 else yh
        base = (b * NZ + lax.rem(z + d, NZ)) * FEAT
        res = []
        for n, tile in enumerate((2 * core, 1, 2 - 2 * core)):
            col = pl.multiple_of(base + tile * HD, HD)
            res.append(pltpu.make_async_copy(w.at[:, pl.ds(col, HD)], wbuf.at[k, :, pl.ds(n * HD, HD)], w_sem.at[k, n]))
        return res

    pair = lax.rem(g + 4, 8)
    mv_slot = [plan[0, g * 2 + m] for m in range(2)]
    mv_arr = [plan[1, g * 2 + m] for m in range(2)]
    in_slot = [plan[0, pair * 2 + m] for m in range(2)]
    in_arr = [plan[1, pair * 2 + m] for m in range(2)]
    mv_row = [jnp.minimum(s, LIVE - 1) for s in mv_slot]

    def pick(m, values):
        return jnp.where(m == 0, values[0], values[1])

    q_copy.wait()
    r, c = iota((16, ROWS), 0), iota((16, ROWS), 1)
    land_pick = one_hot((r < 8) & (c == (r & 3) * SLOTS + LIVE + (r >> 2)))
    for n in range(3):
        land_src[n] = dot(land_pick, ext[n, 0:ROWS]).astype(BF16)
        ext[n, ROWS + 16:256] = jnp.zeros((112, FEAT), BF16)

    live_rows = LIVE * RPS
    r, c = iota((live_rows, ROWS), 0), iota((live_rows, ROWS), 1)
    q_pick = one_hot(c == (r & 3) * SLOTS + (r >> 4))
    spread = dot(q_pick, ext[0, 0:ROWS])
    r, c = iota((live_rows, FEAT), 0), iota((live_rows, FEAT), 1)
    qb[0:live_rows] = jnp.where((c >> 7) == ((r >> 2) & 3), spread, 0.0).astype(BF16)

    r, c = iota((live_rows, ROWS), 0), iota((live_rows, ROWS), 1)
    raw = dot_t(qb[0:live_rows], ext[1, 0:ROWS])
    sn[...] = jnp.where(((c & 31) == (r >> 4)) & ((c >> 5) <= (r & 3)), raw * SCALE, -jnp.inf)

    pl.semaphore_wait(barrier, len(peers))
    land_copy = pltpu.make_async_remote_copy(
        src_ref=land_src, dst_ref=land_dst, send_sem=land_sem.at[0], recv_sem=land_sem.at[1],
        device_id=x_peer, device_id_type=MESH)
    land_copy.start()

    for cp in k_copies:
        cp.wait()
    for k in range(2 * NZ):
        for cp in w_copies(k):
            cp.start()
    lane = iota((RPS, PAGE), 1)

    def cache_scores(i):
        page = jnp.minimum(table[0, i], LIVE_PAGES - 1)
        raw = dot_t(qb[pl.ds(pl.multiple_of(i * RPS, RPS), RPS)], kbuf[page])
        sc[pl.ds(pl.multiple_of(i * RPS, RPS), RPS)] = jnp.where(lane < lens[g * SLOTS + i], raw * SCALE, -jnp.inf)

    def some_scores(n, _):
        for j in range(6):
            cache_scores(n * 6 + j)
        return 0

    lax.fori_loop(0, LIVE // 6, some_scores, 0)

    part = 96

    def soft(n, _):
        at = pl.ds(pl.multiple_of(n * part, part), part)
        a, b = sc[at], sn[at]
        top = jnp.max(jnp.maximum(a, b), axis=1, keepdims=True)
        ea, eb = jnp.exp(a - top), jnp.exp(b - top)
        inv = 1.0 / jnp.sum(ea + eb, axis=1, keepdims=True)
        pc[at] = (ea * inv).astype(BF16)
        pn[at] = (eb * inv).astype(BF16)
        return 0

    lax.fori_loop(0, live_rows // part, soft, 0)

    land_copy.wait()
    for n in range(3):
        ext[n, ROWS:ROWS + 16] = land_dst[n]
    r, c = iota((32, 256), 0), iota((32, 256), 1)
    m, s = r >> 4, r & 3
    early = s < pick(m, mv_arr)
    mv_pick = one_hot((early & (c == s * SLOTS + pick(m, mv_row))) | (~early & (c == ROWS + m * 4 + s)))
    spread = dot(mv_pick, ext[0])
    r, c = iota((32, FEAT), 0), iota((32, FEAT), 1)
    qm = jnp.where((c >> 7) == ((r >> 2) & 3), spread, 0.0).astype(BF16)
    qb[live_rows:] = qm
    r, c = iota((32, 256), 0), iota((32, 256), 1)
    m, s = r >> 4, r & 3
    arr, row = pick(m, mv_arr), pick(m, mv_row)
    u_own, u_land = c >> 5, c & 3
    ok_own = (c < ROWS) & ((c & 31) == row) & (u_own < arr) & (u_own <= s)
    ok_land = (c >= ROWS) & (c < ROWS + 8) & (((c >> 2) & 1) == m) & (u_land >= arr) & (u_land <= s)
    sm = jnp.where(ok_own | ok_land, dot_t(qm, ext[1]) * SCALE, -jnp.inf)
    mv_page = [[jnp.minimum(table[j, mv_row[m]], LIVE_PAGES - 1) for j in range(MAXP)] for m in range(2)]
    for m in range(2):
        q_one = qb[live_rows + m * RPS:live_rows + (m + 1) * RPS]
        for j in range(MAXP):
            raw = dot_t(q_one, kbuf[mv_page[m][j]])
            scm[m * RPS:(m + 1) * RPS, j * PAGE:(j + 1) * PAGE] = jnp.where(
                lane + j * PAGE < lens[g * SLOTS + mv_row[m]], raw * SCALE, -jnp.inf)
    a = scm[...]
    top = jnp.maximum(jnp.max(a, axis=1, keepdims=True), jnp.max(sm, axis=1, keepdims=True))
    ea, eb = jnp.exp(a - top), jnp.exp(sm - top)
    inv = 1.0 / (jnp.sum(ea, axis=1, keepdims=True) + jnp.sum(eb, axis=1, keepdims=True))
    scm[...] = ea * inv
    for cp in v_copies:
        cp.wait()
    om_new = dot((eb * inv).astype(BF16), ext[2])
    c, r = iota((RPS, FEAT), 1), iota((RPS, FEAT), 0)
    diag = (c >> 7) == (r >> 2)
    for m in range(2):
        acc = om_new[m * RPS:(m + 1) * RPS]
        for j in range(MAXP):
            acc = acc + dot(scm[m * RPS:(m + 1) * RPS, j * PAGE:(j + 1) * PAGE].astype(BF16), vbuf[mv_page[m][j]])
        ob[live_rows + m * RPS:live_rows + (m + 1) * RPS] = jnp.where(diag, acc, 0.0).astype(BF16)
    r, c = iota((16, 32), 0), iota((16, 32), 1)
    gather = one_hot(((c >> 4) == (r >> 2)) & ((c & 3) == (r & 3)))
    moved_src[...] = dot(gather, ob[live_rows:]).astype(BF16)
    moved_copy = pltpu.make_async_remote_copy(
        src_ref=moved_src, dst_ref=moved_dst, send_sem=moved_sem.at[0], recv_sem=moved_sem.at[1],
        device_id=x_peer, device_id_type=MESH)
    moved_copy.start()

    on[...] = dot(pn[...], ext[2, 0:ROWS])

    def some_values(n, _):
        for j in range(6):
            i = n * 6 + j
            at = pl.ds(pl.multiple_of(i * RPS, RPS), RPS)
            page = jnp.minimum(table[0, i], LIVE_PAGES - 1)
            acc = on[at] + dot(pc[at], vbuf[page])
            ob[at] = jnp.where(diag, acc, 0.0).astype(BF16)
        return 0

    lax.fori_loop(0, LIVE // 6, some_values, 0)

    r, c = iota((ROWS, 512), 0), iota((ROWS, 512), 1)
    slot, step = r & 31, r >> 5
    src, src_step, m = c >> 4, c & 3, (c >> 4) - LIVE
    stays = (src < LIVE) & (slot == src) & (slot != mv_slot[0]) & (slot != mv_slot[1])
    moves = (src >= LIVE) & (slot == pick(m, mv_slot)) & (step < pick(m, mv_arr))
    keep = one_hot((step == src_step) & (stays | moves))
    total = dot(keep, ob[...])
    moved_copy.wait()
    r, c = iota((ROWS, 16), 0), iota((ROWS, 16), 1)
    slot, step, m = r & 31, r >> 5, (c >> 2) & 1
    lands = (c < 8) & (slot == LIVE + m) & (step == (c & 3)) & (step >= pick(m, in_arr)) & (pick(m, in_slot) < LIVE)
    attn[...] = (total + dot(one_hot(lands), moved_dst[...])).astype(BF16)

    low = iota((64, HD), 1) < 64
    core0 = core == 0

    def project(k):
        for cp in w_copies(k):
            cp.wait()
        res = dot(attn[...], wbuf[k])
        mid_a, mid_b = res[0:64, HD:2 * HD], res[64:ROWS, HD:2 * HD]
        left = jnp.where(low, mid_a, pltpu.roll(mid_b, 64, 1))
        right = jnp.where(low, pltpu.roll(mid_a, 64, 1), mid_b)
        own[k, 0:ROWS] = res[:, 0:HD]
        own[k, ROWS:UNIT] = jnp.where(core0, left, right)
        core_src[k, 0:ROWS] = res[:, 2 * HD:].astype(BF16)
        core_src[k, ROWS:UNIT] = jnp.where(core0, right, left).astype(BF16)

    def core_copy(k):
        return pltpu.make_async_remote_copy(
            src_ref=core_src.at[k], dst_ref=core_dst.at[k], send_sem=core_ssem.at[k], recv_sem=core_rsem.at[k],
            device_id=sibling, device_id_type=MESH)

    def y_copy(k):
        return pltpu.make_async_remote_copy(
            src_ref=y_src.at[k], dst_ref=y_dst.at[k], send_sem=y_ssem.at[k], recv_sem=y_rsem.at[k],
            device_id=y_peer, device_id_type=MESH)

    def z_copy(k):
        return pltpu.make_async_remote_copy(
            src_ref=z_src.at[k], dst_ref=z_dst.at[k], send_sem=z_ssem.at[k], recv_sem=z_rsem.at[k],
            device_id=z_peer(Z_ORDER[k]), device_id_type=MESH)

    def away(k):
        core_copy(k).wait_recv()
        y_src[k] = (own[k] + core_dst[k].astype(F32)).astype(BF16)
        y_copy(k).start()

    for k in range(NZ):
        project(k)
        core_copy(k).start()
        if k >= 2:
            away(k - 2)
    away(NZ - 2)
    away(NZ - 1)
    for k in range(NZ):
        project(NZ + k)
        core_copy(NZ + k).start()

    def home(k):
        core_copy(NZ + k).wait_recv()
        y_copy(k).wait_recv()
        return own[NZ + k] + core_dst[NZ + k].astype(F32) + y_dst[k].astype(F32)

    for k in range(NZ - 1):
        z_src[k] = home(k).astype(BF16)
        z_copy(k).start()
    result = home(NZ - 1)
    for k in range(NZ - 1):
        z_copy(k).wait_recv()
        result = result + z_dst[k].astype(F32)

    side = result[0:ROWS]
    mid = result[ROWS:UNIT]
    first = iota((ROWS, HD), 1) < 64
    mid_left = jnp.concatenate([mid, pltpu.roll(mid, 64, 1)], 0)
    turned = pltpu.roll(side, 64, 1)
    one = jnp.where(core0, side, jnp.where(first, mid_left, turned))
    two = jnp.where(core0, mid_left, turned)
    out[:, 0:HD] = one.astype(BF16)
    out[:, HD:UNIT] = two[:, 0:64].astype(BF16)

    for k in range(2 * NZ):
        core_copy(k).wait_send()
    for k in range(NZ):
        y_copy(k).wait_send()
    for k in range(NZ - 1):
        z_copy(k).wait_send()


def per_device(kv, qkv, w, table, lens, plan):
    vmem, sems = pltpu.VMEM, pltpu.SemaphoreType.DMA
    hbm, smem = pl.BlockSpec(memory_space=pl.ANY), pl.BlockSpec(memory_space=pltpu.SMEM)
    unit = (UNIT, HD)
    res = pl.pallas_call(
        kernel,
        out_shape=jax.ShapeDtypeStruct((ROWS, UNIT), BF16),
        in_specs=[hbm, hbm, hbm, smem, smem, smem],
        out_specs=pl.BlockSpec(memory_space=pltpu.VMEM),
        scratch_shapes=[
            vmem((LIVE_PAGES, PAGE, FEAT), BF16), vmem((LIVE_PAGES, PAGE, FEAT), BF16), vmem((2 * NZ, FEAT, FEAT), BF16),
            vmem((3, 256, FEAT), BF16), vmem((3, 16, FEAT), BF16), vmem((3, 16, FEAT), BF16),
            vmem((16, FEAT), BF16), vmem((16, FEAT), BF16),
            vmem((512, FEAT), BF16), vmem((LIVE * RPS, PAGE), F32), vmem((LIVE * RPS, ROWS), F32),
            vmem((32, MAXP * PAGE), F32), vmem((32, 256), F32),
            vmem((LIVE * RPS, PAGE), BF16), vmem((LIVE * RPS, ROWS), BF16), vmem((LIVE * RPS, FEAT), F32),
            vmem((512, FEAT), BF16), vmem((ROWS, FEAT), BF16),
            vmem((2 * NZ,) + unit, F32), vmem((2 * NZ,) + unit, BF16), vmem((2 * NZ,) + unit, BF16),
            vmem((NZ,) + unit, BF16), vmem((NZ,) + unit, BF16),
            vmem((NZ - 1,) + unit, BF16), vmem((NZ - 1,) + unit, BF16),
            sems((CHUNKS,)), sems((CHUNKS,)), sems((2 * NZ, 3)), sems, sems((2,)), sems((2,)),
            sems((2 * NZ,)), sems((2 * NZ,)), sems((NZ,)), sems((NZ,)), sems((NZ - 1,)), sems((NZ - 1,)),
        ],
        compiler_params=pltpu.CompilerParams(collective_id=0, has_side_effects=True, vmem_limit_bytes=60 << 20),
    )(kv, qkv.reshape(3, ROWS, FEAT), w, table.T, lens, plan.T)
    return res.reshape(STEPS, SLOTS, UNIT)


def solution(mesh):
    return jax.shard_map(
        per_device,
        mesh=mesh,
        in_specs=(P(None, "grp", None, "head"), P(None, None, "grp", "head"), P("head", None), P("grp", None), P(), P()),
        out_specs=P(None, "grp", "head"),
        check_vma=False,
    )
```

```python
import jax
import jax.numpy as jnp
from jax import lax
from jax.experimental import pallas as pl
from jax.experimental.pallas import tpu as pltpu
from jax.sharding import PartitionSpec as P

MESH = pl.DeviceIdType.MESH
HD = 128
HEADS = 3
FEAT = HEADS * HD
STEPS = 4
SLOTS = 32
LIVE = 30
LIVE_PAGES = 36
PAGE = 128
MAXP = 4
ROWS = STEPS * SLOTS
RPS = 16
CHUNKS = 4
NZ = 8
UNIT = 192
F32 = jnp.float32
BF16 = jnp.bfloat16
SCALE = HD ** -0.5


def iota(shape, dim):
    return lax.broadcasted_iota(jnp.int32, shape, dim)


def one_hot(cond):
    return jnp.where(cond, 1.0, 0.0).astype(BF16)


def dot(a, b):
    return jnp.dot(a, b, preferred_element_type=F32)


def dot_t(a, b):
    return lax.dot_general(a, b, (((1,), (1,)), ((), ())), preferred_element_type=F32)


def kernel(kv, qkv, w, table_in, lens_in, plan_in, out,
           table, lens, plan, kbuf, vbuf, wbuf, ext, land_src, land_dst, moved_src, moved_dst,
           qb, sc, sn, scm, pc, pn, on, ob, attn, attn_c,
           own, y_src, y_dst, z_src, z_dst, own_c, yc_src, yc_dst, zc_src, zc_dst,
           i_sem, k_sem, v_sem, w_sem, q_sem, land_sem, moved_sem, core_sem, core_c_sem,
           wp_ssem, wp_rsem, y_ssem, y_rsem, z_ssem, z_rsem, yc_sem, zc_ssem, zc_rsem):
    g = lax.axis_index("grp")
    h = lax.axis_index("head")
    yh, z, core = h // 16, lax.rem(h // 2, NZ), lax.rem(h, 2)
    sibling = (g, h + 1 - 2 * core)
    y_peer = (g, lax.rem(h + 16, 32))
    pair = lax.rem(g + 4, 8)
    x_peer = (pair, h)

    def z_device(t):
        return (g, yh * 16 + t * 2 + core)

    def z_at(k):
        return z if k == NZ - 1 else k + jnp.where(z > k, 0, 1)

    q_copy = pltpu.make_async_copy(qkv, ext.at[:, pl.ds(0, ROWS)], q_sem)
    q_copy.start()
    i_copies = [pltpu.make_async_copy(src, dst, i_sem.at[n])
                for n, (src, dst) in enumerate(((table_in, table), (lens_in, lens), (plan_in, plan)))]
    for cp in i_copies:
        cp.start()
    per = LIVE_PAGES // CHUNKS

    def page_copies(which, buf, sem):
        return [pltpu.make_async_copy(kv.at[which, pl.ds(n * per, per)], buf.at[pl.ds(n * per, per)], sem.at[n])
                for n in range(CHUNKS)]

    k_copies = page_copies(0, kbuf, k_sem)
    v_copies = page_copies(1, vbuf, v_sem)
    for cp in k_copies + v_copies:
        cp.start()

    barrier = pltpu.get_barrier_semaphore()
    peers = [sibling, y_peer] + [z_device(z_at(k)) for k in range(NZ - 1)] + [x_peer]
    for peer in peers:
        pl.semaphore_signal(barrier, inc=1, device_id=peer, device_id_type=MESH)

    def w_columns(k, c):
        b = (1 - yh) if k < NZ else yh
        return w.at[:, pl.ds(pl.multiple_of((b * NZ + z_at(k % NZ)) * FEAT + c * HD, HD), 2 * HD)]

    def w_copy(k):
        return pltpu.make_async_copy(w_columns(k, core), wbuf.at[k, pl.ds(0, FEAT)], w_sem.at[k])

    def w_push(k):
        return pltpu.make_async_remote_copy(
            src_ref=w_columns(k, 1 - core), dst_ref=wbuf.at[k, pl.ds(FEAT, FEAT)], send_sem=wp_ssem.at[k], recv_sem=wp_rsem.at[k],
            device_id=sibling, device_id_type=MESH)

    q_copy.wait()
    r, c = iota((16, ROWS), 0), iota((16, ROWS), 1)
    land_pick = one_hot((r < 8) & (c == (r & 3) * SLOTS + LIVE + (r >> 2)))
    for n in range(3):
        land_src[n] = dot(land_pick, ext[n, 0:ROWS]).astype(BF16)
        ext[n, ROWS + 16:256] = jnp.zeros((112, FEAT), BF16)

    for cp in i_copies:
        cp.wait()
    mv_slot = [plan[0, g * 2 + m] for m in range(2)]
    mv_arr = [plan[1, g * 2 + m] for m in range(2)]
    in_slot = [plan[0, pair * 2 + m] for m in range(2)]
    in_arr = [plan[1, pair * 2 + m] for m in range(2)]
    mv_row = [jnp.minimum(s, LIVE - 1) for s in mv_slot]

    def pick(m, values):
        return jnp.where(m == 0, values[0], values[1])

    live_rows = LIVE * RPS
    r, c = iota((live_rows, ROWS), 0), iota((live_rows, ROWS), 1)
    q_pick = one_hot(c == (r & 3) * SLOTS + (r >> 4))
    spread = dot(q_pick, ext[0, 0:ROWS])
    r, c = iota((live_rows, FEAT), 0), iota((live_rows, FEAT), 1)
    qb[0:live_rows] = jnp.where((c >> 7) == ((r >> 2) & 3), spread, 0.0).astype(BF16)

    r, c = iota((live_rows, ROWS), 0), iota((live_rows, ROWS), 1)
    raw = dot_t(qb[0:live_rows], ext[1, 0:ROWS])
    sn[...] = jnp.where(((c & 31) == (r >> 4)) & ((c >> 5) <= (r & 3)), raw * SCALE, -jnp.inf)

    pl.semaphore_wait(barrier, len(peers))
    land_copy = pltpu.make_async_remote_copy(
        src_ref=land_src, dst_ref=land_dst, send_sem=land_sem.at[0], recv_sem=land_sem.at[1],
        device_id=x_peer, device_id_type=MESH)
    land_copy.start()
    for k in range(2 * NZ):
        w_push(k).start()

    for cp in k_copies:
        cp.wait()
    for k in range(2 * NZ):
        w_copy(k).start()
    lane = iota((RPS, PAGE), 1)

    def cache_scores(i):
        page = jnp.minimum(table[0, i], LIVE_PAGES - 1)
        raw = dot_t(qb[pl.ds(pl.multiple_of(i * RPS, RPS), RPS)], kbuf[page])
        sc[pl.ds(pl.multiple_of(i * RPS, RPS), RPS)] = jnp.where(lane < lens[g * SLOTS + i], raw * SCALE, -jnp.inf)

    def some_scores(n, _):
        for j in range(6):
            cache_scores(n * 6 + j)
        return 0

    lax.fori_loop(0, LIVE // 6, some_scores, 0)

    part = 96

    def soft(n, _):
        at = pl.ds(pl.multiple_of(n * part, part), part)
        a, b = sc[at], sn[at]
        top = jnp.max(jnp.maximum(a, b), axis=1, keepdims=True)
        ea, eb = jnp.exp(a - top), jnp.exp(b - top)
        inv = 1.0 / jnp.sum(ea + eb, axis=1, keepdims=True)
        pc[at] = (ea * inv).astype(BF16)
        pn[at] = (eb * inv).astype(BF16)
        return 0

    lax.fori_loop(0, live_rows // part, soft, 0)

    for cp in v_copies:
        cp.wait()
    c, r = iota((RPS, FEAT), 1), iota((RPS, FEAT), 0)
    diag = (c >> 7) == (r >> 2)
    on[...] = dot(pn[...], ext[2, 0:ROWS])

    def some_values(n, _):
        for j in range(6):
            i = n * 6 + j
            at = pl.ds(pl.multiple_of(i * RPS, RPS), RPS)
            page = jnp.minimum(table[0, i], LIVE_PAGES - 1)
            acc = on[at] + dot(pc[at], vbuf[page])
            ob[at] = jnp.where(diag, acc, 0.0).astype(BF16)
        return 0

    lax.fori_loop(0, LIVE // 6, some_values, 0)

    r, c = iota((ROWS, live_rows), 0), iota((ROWS, live_rows), 1)
    slot = r & 31
    keep = ((r >> 5) == (c & 3)) & (slot == (c >> 4)) & (slot != mv_slot[0]) & (slot != mv_slot[1])
    attn[:, 0:FEAT] = dot(one_hot(keep), ob[0:live_rows]).astype(BF16)
    attn_copy = pltpu.make_async_remote_copy(
        src_ref=attn.at[:, pl.ds(0, FEAT)], dst_ref=attn.at[:, pl.ds(FEAT, FEAT)], send_sem=core_sem.at[0], recv_sem=core_sem.at[1],
        device_id=sibling, device_id_type=MESH)
    attn_copy.start()

    land_copy.wait_recv()
    for n in range(3):
        ext[n, ROWS:ROWS + 16] = land_dst[n]
    r, c = iota((32, 256), 0), iota((32, 256), 1)
    m, s = r >> 4, r & 3
    early = s < pick(m, mv_arr)
    mv_pick = one_hot((early & (c == s * SLOTS + pick(m, mv_row))) | (~early & (c == ROWS + m * 4 + s)))
    spread = dot(mv_pick, ext[0])
    r, c = iota((32, FEAT), 0), iota((32, FEAT), 1)
    qm = jnp.where((c >> 7) == ((r >> 2) & 3), spread, 0.0).astype(BF16)
    qb[live_rows:] = qm
    r, c = iota((32, 256), 0), iota((32, 256), 1)
    m, s = r >> 4, r & 3
    arr, row = pick(m, mv_arr), pick(m, mv_row)
    u_own, u_land = c >> 5, c & 3
    ok_own = (c < ROWS) & ((c & 31) == row) & (u_own < arr) & (u_own <= s)
    ok_land = (c >= ROWS) & (c < ROWS + 8) & (((c >> 2) & 1) == m) & (u_land >= arr) & (u_land <= s)
    sm = jnp.where(ok_own | ok_land, dot_t(qm, ext[1]) * SCALE, -jnp.inf)
    mv_page = [[jnp.minimum(table[j, mv_row[m]], LIVE_PAGES - 1) for j in range(MAXP)] for m in range(2)]
    for m in range(2):
        q_one = qb[live_rows + m * RPS:live_rows + (m + 1) * RPS]
        for j in range(MAXP):
            raw = dot_t(q_one, kbuf[mv_page[m][j]])
            scm[m * RPS:(m + 1) * RPS, j * PAGE:(j + 1) * PAGE] = jnp.where(
                lane + j * PAGE < lens[g * SLOTS + mv_row[m]], raw * SCALE, -jnp.inf)
    a = scm[...]
    top = jnp.maximum(jnp.max(a, axis=1, keepdims=True), jnp.max(sm, axis=1, keepdims=True))
    ea, eb = jnp.exp(a - top), jnp.exp(sm - top)
    inv = 1.0 / (jnp.sum(ea, axis=1, keepdims=True) + jnp.sum(eb, axis=1, keepdims=True))
    scm[...] = ea * inv
    om_new = dot((eb * inv).astype(BF16), ext[2])
    for m in range(2):
        acc = om_new[m * RPS:(m + 1) * RPS]
        for j in range(MAXP):
            acc = acc + dot(scm[m * RPS:(m + 1) * RPS, j * PAGE:(j + 1) * PAGE].astype(BF16), vbuf[mv_page[m][j]])
        ob[live_rows + m * RPS:live_rows + (m + 1) * RPS] = jnp.where(diag, acc, 0.0).astype(BF16)
    r, c = iota((16, 32), 0), iota((16, 32), 1)
    gather = one_hot(((c >> 4) == (r >> 2)) & ((c & 3) == (r & 3)))
    moved = dot(gather, ob[live_rows:])
    moved_src[...] = moved.astype(BF16)
    moved_copy = pltpu.make_async_remote_copy(
        src_ref=moved_src, dst_ref=moved_dst, send_sem=moved_sem.at[0], recv_sem=moved_sem.at[1],
        device_id=x_peer, device_id_type=MESH)
    moved_copy.start()

    low = iota((64, HD), 1) < 64
    core0 = core == 0

    def project(k):
        w_copy(k).wait()
        w_push(k).wait_recv()
        res = dot(attn[...], wbuf[k])
        one, two = res[:, 0:HD], res[:, HD:2 * HD]
        left = jnp.where(low, two[0:64], pltpu.roll(two[64:ROWS], 64, 1))
        right = jnp.where(low, pltpu.roll(one[0:64], 64, 1), one[64:ROWS])
        return jnp.where(core0, one, two), jnp.where(core0, left, right)

    def y_copy(k):
        return pltpu.make_async_remote_copy(
            src_ref=y_src.at[k], dst_ref=y_dst.at[k], send_sem=y_ssem.at[k], recv_sem=y_rsem.at[k],
            device_id=y_peer, device_id_type=MESH)

    def z_copy(k, slot):
        return pltpu.make_async_remote_copy(
            src_ref=z_src.at[k], dst_ref=z_dst.at[slot], send_sem=z_ssem.at[k], recv_sem=z_rsem.at[slot],
            device_id=z_device(z_at(k)), device_id_type=MESH)

    def slot_at(k):
        return z - jnp.where(z > k, 1, 0)

    def send_home(k):
        y_copy(k).wait_recv()
        z_src[k] = (own[k] + y_dst[k].astype(F32)).astype(BF16)
        z_copy(k, slot_at(k)).start()

    attn_copy.wait_recv()
    for k in range(NZ):
        side, mid = project(k)
        y_src[k, 0:ROWS] = side.astype(BF16)
        y_src[k, ROWS:UNIT] = mid.astype(BF16)
        y_copy(k).start()
    for k in range(NZ):
        own[k, 0:ROWS], own[k, ROWS:UNIT] = project(NZ + k)

    moved_copy.wait_recv()
    r = iota((16, FEAT), 0)
    m, s = (r >> 2) & 1, r & 3
    leaves = (r < 8) & (s < pick(m, mv_arr))
    lands = (r < 8) & (s >= pick(m, in_arr)) & (pick(m, in_slot) < LIVE)
    attn_c[:, 0:FEAT] = jnp.where(leaves, moved, jnp.where(lands, moved_dst[...].astype(F32), 0.0)).astype(BF16)
    attn_c_copy = pltpu.make_async_remote_copy(
        src_ref=attn_c.at[:, pl.ds(0, FEAT)], dst_ref=attn_c.at[:, pl.ds(FEAT, FEAT)],
        send_sem=core_c_sem.at[0], recv_sem=core_c_sem.at[1], device_id=sibling, device_id_type=MESH)
    attn_c_copy.start()
    yc_copy = pltpu.make_async_remote_copy(
        src_ref=yc_src, dst_ref=yc_dst, send_sem=yc_sem.at[0], recv_sem=yc_sem.at[1], device_id=y_peer, device_id_type=MESH)

    def zc_copy(k, slot):
        return pltpu.make_async_remote_copy(
            src_ref=zc_src.at[k], dst_ref=zc_dst.at[slot], send_sem=zc_ssem.at[k], recv_sem=zc_rsem.at[slot],
            device_id=z_device(z_at(k)), device_id_type=MESH)

    def project_c(k):
        res = dot(attn_c[...], wbuf[k])
        one, two = res[0:8, 0:HD], res[0:8, HD:2 * HD]
        return jnp.concatenate([jnp.where(core0, one, two), jnp.where(core0, two, one)], 0)

    for k in range(2):
        send_home(k)
    attn_c_copy.wait_recv()
    for k in range(NZ):
        yc_src[k] = project_c(k).astype(BF16)
    yc_copy.start()
    for k in range(2, 4):
        send_home(k)
    for k in range(NZ):
        own_c[k] = project_c(NZ + k)
    for k in range(4, 6):
        send_home(k)
    yc_copy.wait_recv()
    own_c[...] = own_c[...] + yc_dst[...].astype(F32)
    for k in range(NZ - 1):
        zc_src[k] = own_c[k].astype(BF16)
    for k in range(NZ - 1):
        zc_copy(k, slot_at(k)).start()
    send_home(6)
    y_copy(NZ - 1).wait_recv()
    total = own[NZ - 1] + y_dst[NZ - 1].astype(F32)
    total_c = own_c[NZ - 1]
    for k in range(NZ - 1):
        z_copy(0, k).wait_recv()
        total = total + z_dst[k].astype(F32)
    for k in range(NZ - 1):
        zc_copy(0, k).wait_recv()
        total_c = total_c + zc_dst[k].astype(F32)

    def columns(side, middle, first):
        turned = pltpu.roll(side, 64, 1)
        return jnp.where(core0, side, jnp.where(first, middle, turned)), jnp.where(core0, middle, turned)

    mid = total[ROWS:UNIT]
    one, two = columns(total[0:ROWS], jnp.concatenate([mid, pltpu.roll(mid, 64, 1)], 0), iota((ROWS, HD), 1) < 64)
    mid = total_c[8:16]
    one_c, two_c = columns(total_c[0:8], jnp.where(core0, mid, pltpu.roll(mid, 64, 1)), iota((8, HD), 1) < 64)
    rest = jnp.zeros((8, HD), F32)
    r, c = iota((ROWS, 16), 0), iota((ROWS, 16), 1)
    slot, step, m = r & 31, r >> 5, (c >> 2) & 1
    lands = (slot == LIVE + m) & (step >= pick(m, in_arr)) & (pick(m, in_slot) < LIVE)
    leaves = (slot == pick(m, mv_slot)) & (step < pick(m, mv_arr))
    place = one_hot((c < 8) & (step == (c & 3)) & (lands | leaves))
    one = one + dot(place, jnp.concatenate([one_c, rest], 0).astype(BF16))
    two = two + dot(place, jnp.concatenate([two_c, rest], 0).astype(BF16))
    out[:, 0:HD] = one.astype(BF16)
    out[:, HD:UNIT] = two[:, 0:64].astype(BF16)

    for cp in (land_copy, attn_copy, moved_copy, attn_c_copy, yc_copy):
        cp.wait_send()
    for k in range(2 * NZ):
        w_push(k).wait_send()
    for k in range(NZ):
        y_copy(k).wait_send()
    for k in range(NZ - 1):
        z_copy(k, 0).wait_send()
        zc_copy(k, 0).wait_send()


def per_device(kv, qkv, w, table, lens, plan):
    vmem, sems = pltpu.VMEM, pltpu.SemaphoreType.DMA
    hbm = pl.BlockSpec(memory_space=pltpu.HBM)
    unit = (UNIT, HD)
    res = pl.pallas_call(
        kernel,
        out_shape=jax.ShapeDtypeStruct((ROWS, UNIT), BF16),
        in_specs=[hbm] * 6,
        out_specs=pl.BlockSpec(memory_space=pltpu.VMEM),
        scratch_shapes=[
            pltpu.SMEM((MAXP, SLOTS), jnp.int32), pltpu.SMEM(lens.shape, jnp.int32), pltpu.SMEM(plan.shape[::-1], jnp.int32),
            vmem((LIVE_PAGES, PAGE, FEAT), BF16), vmem((LIVE_PAGES, PAGE, FEAT), BF16), vmem((2 * NZ, 2 * FEAT, 2 * HD), BF16),
            vmem((3, 256, FEAT), BF16), vmem((3, 16, FEAT), BF16), vmem((3, 16, FEAT), BF16),
            vmem((16, FEAT), BF16), vmem((16, FEAT), BF16),
            vmem((512, FEAT), BF16), vmem((LIVE * RPS, PAGE), F32), vmem((LIVE * RPS, ROWS), F32), vmem((32, MAXP * PAGE), F32),
            vmem((LIVE * RPS, PAGE), BF16), vmem((LIVE * RPS, ROWS), BF16), vmem((LIVE * RPS, FEAT), F32),
            vmem((512, FEAT), BF16), vmem((ROWS, 2 * FEAT), BF16), vmem((16, 2 * FEAT), BF16),
            vmem((NZ,) + unit, F32), vmem((NZ,) + unit, BF16), vmem((NZ,) + unit, BF16),
            vmem((NZ - 1,) + unit, BF16), vmem((NZ - 1,) + unit, BF16),
            vmem((NZ, 16, HD), F32), vmem((NZ, 16, HD), BF16), vmem((NZ, 16, HD), BF16),
            vmem((NZ - 1, 16, HD), BF16), vmem((NZ - 1, 16, HD), BF16),
            sems((3,)), sems((CHUNKS,)), sems((CHUNKS,)), sems((2 * NZ,)), sems, sems((2,)), sems((2,)), sems((2,)), sems((2,)),
            sems((2 * NZ,)), sems((2 * NZ,)), sems((NZ,)), sems((NZ,)), sems((NZ - 1,)), sems((NZ - 1,)),
            sems((2,)), sems((NZ - 1,)), sems((NZ - 1,)),
        ],
        compiler_params=pltpu.CompilerParams(collective_id=0, has_side_effects=True, vmem_limit_bytes=60 << 20),
    )(kv, qkv.reshape(3, ROWS, FEAT), w, table.T, lens, plan.T)
    return res.reshape(STEPS, SLOTS, UNIT)


def solution(mesh):
    return jax.shard_map(
        per_device,
        mesh=mesh,
        in_specs=(P(None, "grp", None, "head"), P(None, None, "grp", "head"), P("head", None), P("grp", None), P(), P()),
        out_specs=P(None, "grp", "head"),
        check_vma=False,
    )
```

```python
import jax
import jax.numpy as jnp
from jax import lax
from jax.experimental import pallas as pl
from jax.experimental.pallas import tpu as pltpu
from jax.sharding import PartitionSpec as P

MESH = pl.DeviceIdType.MESH
HD = 128
HEADS = 3
FEAT = HEADS * HD
STEPS = 4
SLOTS = 32
LIVE = 30
LIVE_PAGES = 36
PAGE = 128
MAXP = 4
ROWS = STEPS * SLOTS
RPS = 16
CHUNKS = 4
NZ = 8
Y_FIRST = 5
FIRST_Z = (0, 1)
Z_ORDER = [[t for t in FIRST_Z if t != n] + sorted((t for t in range(NZ) if t != n and t not in FIRST_Z),
                                                   key=lambda t: -min((t - n) % NZ, (n - t) % NZ)) for n in range(NZ)]
UNIT = 192
F32 = jnp.float32
BF16 = jnp.bfloat16
SCALE = HD ** -0.5


def iota(shape, dim):
    return lax.broadcasted_iota(jnp.int32, shape, dim)


def one_hot(cond):
    return jnp.where(cond, 1.0, 0.0).astype(BF16)


def dot(a, b):
    return jnp.dot(a, b, preferred_element_type=F32)


def dot_t(a, b):
    return lax.dot_general(a, b, (((1,), (1,)), ((), ())), preferred_element_type=F32)


def kernel(kv, qkv, w, table_in, lens_in, plan_in, out,
           table, lens, plan, kbuf, vbuf, wbuf, ext, land_src, land_dst, moved_src, moved_dst,
           qb, sc, sn, scm, pc, pn, on, ob, attn, attn_c,
           own, y_src, y_dst, z_src, z_dst, yc_src, yc_dst, zc_src, zc_dst,
           i_sem, k_sem, v_sem, w_sem, q_sem, land_sem, moved_ssem, moved_rsem, core_sem,
           wp_ssem, wp_rsem, y_ssem, y_rsem, z_ssem, z_rsem, yc_ssem, yc_rsem, zc_ssem, zc_rsem, above_sem):
    g = lax.axis_index("grp")
    h = lax.axis_index("head")
    yh, z, core = h // 16, lax.rem(h // 2, NZ), lax.rem(h, 2)
    sibling = (g, h + 1 - 2 * core)
    y_peer = (g, lax.rem(h + 16, 32))
    pair = lax.rem(g + 4, 8)
    x_peer = (pair, h)

    def z_device(t):
        return (g, yh * 16 + t * 2 + core)

    def z_at(k):
        if k == NZ - 1:
            return z
        t = Z_ORDER[0][k]
        for n in range(1, NZ):
            t = jnp.where(z == n, Z_ORDER[n][k], t)
        return t

    q_copy = pltpu.make_async_copy(qkv, ext.at[:, pl.ds(0, ROWS)], q_sem)
    q_copy.start()
    i_copies = [pltpu.make_async_copy(src, dst, i_sem.at[n])
                for n, (src, dst) in enumerate(((table_in, table), (lens_in, lens), (plan_in, plan)))]
    for cp in i_copies:
        cp.start()
    per = LIVE_PAGES // CHUNKS

    def page_copies(which, buf, sem):
        return [pltpu.make_async_copy(kv.at[which, pl.ds(n * per, per)], buf.at[pl.ds(n * per, per)], sem.at[n])
                for n in range(CHUNKS)]

    k_copies = page_copies(0, kbuf, k_sem)
    v_copies = page_copies(1, vbuf, v_sem)
    for cp in k_copies + v_copies:
        cp.start()

    barrier = pltpu.get_barrier_semaphore()
    x_sibling = (pair, h + 1 - 2 * core)
    near = (sibling, y_peer, x_peer, x_sibling)
    for peer in near:
        pl.semaphore_signal(barrier, inc=1, device_id=peer, device_id_type=MESH)

    def greet_above(t, _):
        pl.semaphore_signal(barrier, inc=1, device_id=z_device(t), device_id_type=MESH)
        return 0

    def answer_below(t, _):
        pl.semaphore_signal(above_sem, inc=1, device_id=z_device(t), device_id_type=MESH)
        return 0

    lax.fori_loop(z + 1, NZ, greet_above, 0)

    def w_columns(k, c):
        b = (1 - yh) if k < NZ else yh
        return w.at[:, pl.ds(pl.multiple_of((b * NZ + z_at(k % NZ)) * FEAT + c * HD, HD), 2 * HD)]

    def w_copy(k):
        return pltpu.make_async_copy(w_columns(k, core), wbuf.at[k, pl.ds(0, FEAT)], w_sem.at[k])

    def w_push(k):
        return pltpu.make_async_remote_copy(
            src_ref=w_columns(k, 1 - core), dst_ref=wbuf.at[k, pl.ds(FEAT, FEAT)], send_sem=wp_ssem.at[k], recv_sem=wp_rsem.at[k],
            device_id=sibling, device_id_type=MESH)

    q_copy.wait()
    r, c = iota((16, ROWS), 0), iota((16, ROWS), 1)
    land_pick = one_hot((r < 8) & (c == (r & 3) * SLOTS + LIVE + (r >> 2)))
    for n in range(3):
        land_src[n] = dot(land_pick, ext[n, 0:ROWS]).astype(BF16)
        ext[n, ROWS + 16:256] = jnp.zeros((112, FEAT), BF16)

    for cp in i_copies:
        cp.wait()
    mv_slot = [plan[0, g * 2 + m] for m in range(2)]
    mv_arr = [plan[1, g * 2 + m] for m in range(2)]
    in_slot = [plan[0, pair * 2 + m] for m in range(2)]
    in_arr = [plan[1, pair * 2 + m] for m in range(2)]
    mv_row = [jnp.minimum(s, LIVE - 1) for s in mv_slot]

    def pick(m, values):
        return jnp.where(m == 0, values[0], values[1])

    live_rows = LIVE * RPS
    r, c = iota((live_rows, ROWS), 0), iota((live_rows, ROWS), 1)
    q_pick = one_hot(c == (r & 3) * SLOTS + (r >> 4))
    spread = dot(q_pick, ext[0, 0:ROWS])
    r, c = iota((live_rows, FEAT), 0), iota((live_rows, FEAT), 1)
    qb[0:live_rows] = jnp.where((c >> 7) == ((r >> 2) & 3), spread, 0.0).astype(BF16)

    pl.semaphore_wait(barrier, len(near) + z)
    land_copy = pltpu.make_async_remote_copy(
        src_ref=land_src, dst_ref=land_dst, send_sem=land_sem.at[0], recv_sem=land_sem.at[1],
        device_id=x_peer, device_id_type=MESH)
    land_copy.start()
    for k in range(2 * NZ):
        w_push(k).start()
    lax.fori_loop(0, z, answer_below, 0)

    r, c = iota((live_rows, ROWS), 0), iota((live_rows, ROWS), 1)
    raw = dot_t(qb[0:live_rows], ext[1, 0:ROWS])
    sn[...] = jnp.where(((c & 31) == (r >> 4)) & ((c >> 5) <= (r & 3)), raw * SCALE, -jnp.inf)

    for cp in k_copies:
        cp.wait()
    for k in range(2 * NZ):
        w_copy(k).start()
    lane = iota((RPS, PAGE), 1)

    def cache_scores(i):
        page = jnp.minimum(table[0, i], LIVE_PAGES - 1)
        raw = dot_t(qb[i * RPS:(i + 1) * RPS], kbuf[page])
        sc[i * RPS:(i + 1) * RPS] = jnp.where(lane < lens[g * SLOTS + i], raw * SCALE, -jnp.inf)

    for i in range(LIVE):
        cache_scores(i)

    part = 240

    def soft(n, _):
        at = pl.ds(pl.multiple_of(n * part, part), part)
        a, b = sc[at], sn[at]
        top = jnp.max(jnp.maximum(a, b), axis=1, keepdims=True)
        ea, eb = jnp.exp(a - top), jnp.exp(b - top)
        inv = 1.0 / jnp.sum(ea + eb, axis=1, keepdims=True)
        pc[at] = (ea * inv).astype(BF16)
        pn[at] = (eb * inv).astype(BF16)
        return 0

    lax.fori_loop(0, live_rows // part, soft, 0)

    for cp in v_copies:
        cp.wait()
    c, r = iota((RPS, FEAT), 1), iota((RPS, FEAT), 0)
    diag = (c >> 7) == (r >> 2)
    on[...] = dot(pn[...], ext[2, 0:ROWS])

    for i in range(LIVE):
        at = pl.ds(i * RPS, RPS)
        page = jnp.minimum(table[0, i], LIVE_PAGES - 1)
        acc = on[at] + dot(pc[at], vbuf[page])
        ob[at] = jnp.where(diag, acc, 0.0).astype(BF16)

    r, c = iota((ROWS, live_rows), 0), iota((ROWS, live_rows), 1)
    slot = r & 31
    keep = ((r >> 5) == (c & 3)) & (slot == (c >> 4)) & (slot != mv_slot[0]) & (slot != mv_slot[1])
    attn[:, 0:FEAT] = dot(one_hot(keep), ob[0:live_rows]).astype(BF16)
    attn_copy = pltpu.make_async_remote_copy(
        src_ref=attn.at[:, pl.ds(0, FEAT)], dst_ref=attn.at[:, pl.ds(FEAT, FEAT)], send_sem=core_sem.at[0], recv_sem=core_sem.at[1],
        device_id=sibling, device_id_type=MESH)
    attn_copy.start()

    land_copy.wait_recv()
    for n in range(3):
        ext[n, ROWS:ROWS + 16] = land_dst[n]
    r, c = iota((32, 256), 0), iota((32, 256), 1)
    m, s = r >> 4, r & 3
    early = s < pick(m, mv_arr)
    mv_pick = one_hot((early & (c == s * SLOTS + pick(m, mv_row))) | (~early & (c == ROWS + m * 4 + s)))
    spread = dot(mv_pick, ext[0])
    r, c = iota((32, FEAT), 0), iota((32, FEAT), 1)
    qm = jnp.where((c >> 7) == ((r >> 2) & 3), spread, 0.0).astype(BF16)
    qb[live_rows:] = qm
    r, c = iota((32, 256), 0), iota((32, 256), 1)
    m, s = r >> 4, r & 3
    arr, row = pick(m, mv_arr), pick(m, mv_row)
    u_own, u_land = c >> 5, c & 3
    ok_own = (c < ROWS) & ((c & 31) == row) & (u_own < arr) & (u_own <= s)
    ok_land = (c >= ROWS) & (c < ROWS + 8) & (((c >> 2) & 1) == m) & (u_land >= arr) & (u_land <= s)
    sm = jnp.where(ok_own | ok_land, dot_t(qm, ext[1]) * SCALE, -jnp.inf)
    mv_page = [[jnp.minimum(table[j, mv_row[m]], LIVE_PAGES - 1) for j in range(MAXP)] for m in range(2)]
    for m in range(2):
        q_one = qb[live_rows + m * RPS:live_rows + (m + 1) * RPS]
        for j in range(MAXP):
            raw = dot_t(q_one, kbuf[mv_page[m][j]])
            scm[m * RPS:(m + 1) * RPS, j * PAGE:(j + 1) * PAGE] = jnp.where(
                lane + j * PAGE < lens[g * SLOTS + mv_row[m]], raw * SCALE, -jnp.inf)
    a = scm[...]
    top = jnp.maximum(jnp.max(a, axis=1, keepdims=True), jnp.max(sm, axis=1, keepdims=True))
    ea, eb = jnp.exp(a - top), jnp.exp(sm - top)
    inv = 1.0 / (jnp.sum(ea, axis=1, keepdims=True) + jnp.sum(eb, axis=1, keepdims=True))
    scm[...] = ea * inv
    om_new = dot((eb * inv).astype(BF16), ext[2])
    for m in range(2):
        acc = om_new[m * RPS:(m + 1) * RPS]
        for j in range(MAXP):
            acc = acc + dot(scm[m * RPS:(m + 1) * RPS, j * PAGE:(j + 1) * PAGE].astype(BF16), vbuf[mv_page[m][j]])
        ob[live_rows + m * RPS:live_rows + (m + 1) * RPS] = jnp.where(diag, acc, 0.0).astype(BF16)
    r, c = iota((16, 32), 0), iota((16, 32), 1)
    gather = one_hot(((c >> 4) == (r >> 2)) & ((c & 3) == (r & 3)))
    moved = dot(gather, ob[live_rows:])
    moved_src[...] = moved.astype(BF16)
    moved_copies = [pltpu.make_async_remote_copy(
        src_ref=moved_src, dst_ref=moved_dst.at[n], send_sem=moved_ssem.at[n], recv_sem=moved_rsem.at[n],
        device_id=peer, device_id_type=MESH) for n, peer in enumerate((x_peer, x_sibling, sibling))]
    for cp in moved_copies:
        cp.start()

    low = iota((64, HD), 1) < 64
    core0 = core == 0

    def project(k):
        w_copy(k).wait()
        w_push(k).wait_recv()
        res = dot(attn[...], wbuf[k])
        one, two = res[:, 0:HD], res[:, HD:2 * HD]
        left = jnp.where(low, two[0:64], pltpu.roll(two[64:ROWS], 64, 1))
        right = jnp.where(low, pltpu.roll(one[0:64], 64, 1), one[64:ROWS])
        return jnp.where(core0, one, two), jnp.where(core0, left, right)

    def y_copy(k):
        return pltpu.make_async_remote_copy(
            src_ref=y_src.at[k], dst_ref=y_dst.at[k], send_sem=y_ssem.at[k], recv_sem=y_rsem.at[k],
            device_id=y_peer, device_id_type=MESH)

    def z_copy(k, slot):
        return pltpu.make_async_remote_copy(
            src_ref=z_src.at[k], dst_ref=z_dst.at[slot], send_sem=z_ssem.at[k], recv_sem=z_rsem.at[slot],
            device_id=z_device(z_at(k)), device_id_type=MESH)

    def slot_at(k):
        return z - jnp.where(z > z_at(k), 1, 0)

    def send_home(k):
        y_copy(k).wait_recv()
        z_src[k] = (own[k] + y_dst[k].astype(F32)).astype(BF16)
        z_copy(k, slot_at(k)).start()

    attn_copy.wait_recv()
    for k in range(NZ):
        side, mid = project(k)
        y_src[k, 0:ROWS] = side.astype(BF16)
        y_src[k, ROWS:UNIT] = mid.astype(BF16)
        if k < Y_FIRST:
            y_copy(k).start()
    for k in range(NZ):
        own[k, 0:ROWS], own[k, ROWS:UNIT] = project(NZ + k)

    for cp in moved_copies:
        cp.wait_recv()
    r = iota((16, FEAT), 0)
    m, s = (r >> 2) & 1, r & 3
    leaves = (r < 8) & (s < pick(m, mv_arr))
    lands = (r < 8) & (s >= pick(m, in_arr)) & (pick(m, in_slot) < LIVE)
    for n, mine in enumerate((moved, moved_dst[2].astype(F32))):
        attn_c[:, n * FEAT:(n + 1) * FEAT] = jnp.where(
            leaves, mine, jnp.where(lands, moved_dst[n].astype(F32), 0.0)).astype(BF16)

    def yc_copy(k, slot):
        return pltpu.make_async_remote_copy(
            src_ref=yc_src.at[k], dst_ref=yc_dst.at[slot], send_sem=yc_ssem.at[k], recv_sem=yc_rsem.at[slot],
            device_id=(g, (1 - yh) * 16 + z_at(k) * 2 + core), device_id_type=MESH)

    def zc_copy(k, slot):
        return pltpu.make_async_remote_copy(
            src_ref=zc_src.at[k], dst_ref=zc_dst.at[slot], send_sem=zc_ssem.at[k], recv_sem=zc_rsem.at[slot],
            device_id=z_device(z_at(k)), device_id_type=MESH)

    def project_c(k):
        res = dot(attn_c[...], wbuf[k])
        one, two = res[0:8, 0:HD], res[0:8, HD:2 * HD]
        return jnp.concatenate([jnp.where(core0, one, two), jnp.where(core0, two, one)], 0)

    @pl.when(z < NZ - 1)
    def _():
        pl.semaphore_wait(above_sem, NZ - 1 - z)

    send_home(0)
    for k in range(NZ):
        yc_src[k] = project_c(k).astype(BF16)
    for k in range(NZ):
        yc_copy(k, z).start()
    for k in range(Y_FIRST, NZ):
        y_copy(k).start()
    for k in range(NZ - 1):
        zc_src[k] = project_c(NZ + k).astype(BF16)
    for k in range(NZ - 1):
        zc_copy(k, slot_at(k)).start()
    total_c = project_c(2 * NZ - 1)
    for k in range(1, NZ - 1):
        send_home(k)
    y_copy(NZ - 1).wait_recv()
    total = own[NZ - 1] + y_dst[NZ - 1].astype(F32)
    for k in range(NZ - 1):
        z_copy(0, k).wait_recv()
        total = total + z_dst[k].astype(F32)
    for k in range(NZ - 1):
        zc_copy(0, k).wait_recv()
        total_c = total_c + zc_dst[k].astype(F32)
    for k in range(NZ):
        yc_copy(0, k).wait_recv()
        total_c = total_c + yc_dst[k].astype(F32)

    def columns(side, middle, first):
        turned = pltpu.roll(side, 64, 1)
        return jnp.where(core0, side, jnp.where(first, middle, turned)), jnp.where(core0, middle, turned)

    mid = total[ROWS:UNIT]
    one, two = columns(total[0:ROWS], jnp.concatenate([mid, pltpu.roll(mid, 64, 1)], 0), iota((ROWS, HD), 1) < 64)
    mid = total_c[8:16]
    one_c, two_c = columns(total_c[0:8], jnp.where(core0, mid, pltpu.roll(mid, 64, 1)), iota((8, HD), 1) < 64)
    rest = jnp.zeros((8, HD), F32)
    r, c = iota((ROWS, 16), 0), iota((ROWS, 16), 1)
    slot, step, m = r & 31, r >> 5, (c >> 2) & 1
    lands = (slot == LIVE + m) & (step >= pick(m, in_arr)) & (pick(m, in_slot) < LIVE)
    leaves = (slot == pick(m, mv_slot)) & (step < pick(m, mv_arr))
    place = one_hot((c < 8) & (step == (c & 3)) & (lands | leaves))
    one = one + dot(place, jnp.concatenate([one_c, rest], 0).astype(BF16))
    two = two + dot(place, jnp.concatenate([two_c, rest], 0).astype(BF16))
    out[:, 0:HD] = one.astype(BF16)
    out[:, HD:UNIT] = two[:, 0:64].astype(BF16)

    for cp in [land_copy, attn_copy] + moved_copies:
        cp.wait_send()
    for k in range(2 * NZ):
        w_push(k).wait_send()
    for k in range(NZ):
        y_copy(k).wait_send()
        yc_copy(k, 0).wait_send()
    for k in range(NZ - 1):
        z_copy(k, 0).wait_send()
        zc_copy(k, 0).wait_send()


def per_device(kv, qkv, w, table, lens, plan):
    vmem, sems = pltpu.VMEM, pltpu.SemaphoreType.DMA
    hbm = pl.BlockSpec(memory_space=pltpu.HBM)
    unit = (UNIT, HD)
    res = pl.pallas_call(
        kernel,
        out_shape=jax.ShapeDtypeStruct((ROWS, UNIT), BF16),
        in_specs=[hbm] * 6,
        out_specs=pl.BlockSpec(memory_space=pltpu.VMEM),
        scratch_shapes=[
            pltpu.SMEM((MAXP, SLOTS), jnp.int32), pltpu.SMEM(lens.shape, jnp.int32), pltpu.SMEM(plan.shape[::-1], jnp.int32),
            vmem((LIVE_PAGES, PAGE, FEAT), BF16), vmem((LIVE_PAGES, PAGE, FEAT), BF16), vmem((2 * NZ, 2 * FEAT, 2 * HD), BF16),
            vmem((3, 256, FEAT), BF16), vmem((3, 16, FEAT), BF16), vmem((3, 16, FEAT), BF16),
            vmem((16, FEAT), BF16), vmem((3, 16, FEAT), BF16),
            vmem((512, FEAT), BF16), vmem((LIVE * RPS, PAGE), F32), vmem((LIVE * RPS, ROWS), F32), vmem((32, MAXP * PAGE), F32),
            vmem((LIVE * RPS, PAGE), BF16), vmem((LIVE * RPS, ROWS), BF16), vmem((LIVE * RPS, FEAT), F32),
            vmem((512, FEAT), BF16), vmem((ROWS, 2 * FEAT), BF16), vmem((16, 2 * FEAT), BF16),
            vmem((NZ,) + unit, F32), vmem((NZ,) + unit, BF16), vmem((NZ,) + unit, BF16),
            vmem((NZ - 1,) + unit, BF16), vmem((NZ - 1,) + unit, BF16),
            vmem((NZ, 16, HD), BF16), vmem((NZ, 16, HD), BF16),
            vmem((NZ - 1, 16, HD), BF16), vmem((NZ - 1, 16, HD), BF16),
            sems((3,)), sems((CHUNKS,)), sems((CHUNKS,)), sems((2 * NZ,)), sems, sems((2,)), sems((3,)), sems((3,)), sems((2,)),
            sems((2 * NZ,)), sems((2 * NZ,)), sems((NZ,)), sems((NZ,)), sems((NZ - 1,)), sems((NZ - 1,)),
            sems((NZ,)), sems((NZ,)), sems((NZ - 1,)), sems((NZ - 1,)), pltpu.SemaphoreType.REGULAR,
        ],
        compiler_params=pltpu.CompilerParams(collective_id=0, has_side_effects=True, vmem_limit_bytes=60 << 20),
    )(kv, qkv.reshape(3, ROWS, FEAT), w, table.T, lens, plan.T)
    return res.reshape(STEPS, SLOTS, UNIT)


def solution(mesh):
    return jax.shard_map(
        per_device,
        mesh=mesh,
        in_specs=(P(None, "grp", None, "head"), P(None, None, "grp", "head"), P("head", None), P("grp", None), P(), P()),
        out_specs=P(None, "grp", "head"),
        check_vma=False,
    )
```

```python
import jax
import jax.numpy as jnp
from jax import lax
from jax.experimental import pallas as pl
from jax.experimental.pallas import tpu as pltpu
from jax.sharding import PartitionSpec as P

MESH = pl.DeviceIdType.MESH
HD = 128
HEADS = 3
FEAT = HEADS * HD
STEPS = 4
SLOTS = 32
LIVE = 30
LIVE_PAGES = 36
PAGE = 128
MAXP = 4
ROWS = STEPS * SLOTS
RPS = 16
CHUNKS = 1
NZ = 8
FIRST_Z = (0, 1)
Z_ORDER = [[t for t in FIRST_Z if t != n] + sorted((t for t in range(NZ) if t != n and t not in FIRST_Z),
                                                   key=lambda t: -min((t - n) % NZ, (n - t) % NZ)) for n in range(NZ)]
UNIT = 192
F32 = jnp.float32
BF16 = jnp.bfloat16
SCALE = HD ** -0.5


def iota(shape, dim):
    return lax.broadcasted_iota(jnp.int32, shape, dim)


def one_hot(cond):
    return jnp.where(cond, 1.0, 0.0).astype(BF16)


def dot(a, b):
    return jnp.dot(a, b, preferred_element_type=F32)


def dot_t(a, b):
    return lax.dot_general(a, b, (((1,), (1,)), ((), ())), preferred_element_type=F32)


def kernel(kv, qkv, w, table_in, lens_in, plan_in, out,
           table, lens, plan, kbuf, vbuf, wbuf, ext, land_src, land_dst, moved_src, moved_dst,
           qb, sc, sn, scm, pc, pn, on, ob, attn, attn_c,
           own, y_src, y_dst, z_src, z_dst, yc_src, yc_dst, zc_src, zc_dst,
           i_sem, k_sem, v_sem, w_sem, q_sem, land_sem, moved_ssem, moved_rsem, core_sem,
           wp_ssem, wp_rsem, y_ssem, y_rsem, z_ssem, z_rsem, yc_ssem, yc_rsem, zc_ssem, zc_rsem, above_sem):
    g = lax.axis_index("grp")
    h = lax.axis_index("head")
    yh, z, core = h // 16, lax.rem(h // 2, NZ), lax.rem(h, 2)
    sibling = (g, h + 1 - 2 * core)
    y_peer = (g, lax.rem(h + 16, 32))
    pair = lax.rem(g + 4, 8)
    x_peer = (pair, h)

    def z_device(t):
        return (g, yh * 16 + t * 2 + core)

    def z_at(k):
        if k == NZ - 1:
            return z
        t = Z_ORDER[0][k]
        for n in range(1, NZ):
            t = jnp.where(z == n, Z_ORDER[n][k], t)
        return t

    q_copy = pltpu.make_async_copy(qkv, ext.at[:, pl.ds(0, ROWS)], q_sem)
    q_copy.start()
    i_copies = [pltpu.make_async_copy(src, dst, i_sem.at[n])
                for n, (src, dst) in enumerate(((table_in, table), (lens_in, lens), (plan_in, plan)))]
    for cp in i_copies:
        cp.start()
    per = LIVE_PAGES // CHUNKS

    def page_copies(which, buf, sem):
        return [pltpu.make_async_copy(kv.at[which, pl.ds(n * per, per)], buf.at[pl.ds(n * per, per)], sem.at[n])
                for n in range(CHUNKS)]

    k_copies = page_copies(0, kbuf, k_sem)
    v_copies = page_copies(1, vbuf, v_sem)
    for cp in k_copies + v_copies:
        cp.start()

    barrier = pltpu.get_barrier_semaphore()
    x_sibling = (pair, h + 1 - 2 * core)
    near = (sibling, y_peer, x_peer, x_sibling)
    for peer in near:
        pl.semaphore_signal(barrier, inc=1, device_id=peer, device_id_type=MESH)

    def greet_above(t, _):
        pl.semaphore_signal(barrier, inc=1, device_id=z_device(t), device_id_type=MESH)
        return 0

    def answer_below(t, _):
        pl.semaphore_signal(above_sem, inc=1, device_id=z_device(t), device_id_type=MESH)
        return 0

    lax.fori_loop(z + 1, NZ, greet_above, 0)

    def w_columns(k, c):
        b = (1 - yh) if k < NZ else yh
        return w.at[:, pl.ds(pl.multiple_of((b * NZ + z_at(k % NZ)) * FEAT + c * HD, HD), 2 * HD)]

    def w_copy(k):
        return pltpu.make_async_copy(w_columns(k, core), wbuf.at[k, pl.ds(0, FEAT)], w_sem.at[k])

    def w_push(k):
        return pltpu.make_async_remote_copy(
            src_ref=w_columns(k, 1 - core), dst_ref=wbuf.at[k, pl.ds(FEAT, FEAT)], send_sem=wp_ssem.at[k], recv_sem=wp_rsem.at[k],
            device_id=sibling, device_id_type=MESH)

    q_copy.wait()
    r, c = iota((16, ROWS), 0), iota((16, ROWS), 1)
    land_pick = one_hot((r < 8) & (c == (r & 3) * SLOTS + LIVE + (r >> 2)))
    for n in range(3):
        land_src[n] = dot(land_pick, ext[n, 0:ROWS]).astype(BF16)
        ext[n, ROWS + 16:256] = jnp.zeros((112, FEAT), BF16)

    for cp in i_copies:
        cp.wait()
    mv_slot = [plan[0, g * 2 + m] for m in range(2)]
    mv_arr = [plan[1, g * 2 + m] for m in range(2)]
    in_slot = [plan[0, pair * 2 + m] for m in range(2)]
    in_arr = [plan[1, pair * 2 + m] for m in range(2)]
    mv_row = [jnp.minimum(s, LIVE - 1) for s in mv_slot]

    def pick(m, values):
        return jnp.where(m == 0, values[0], values[1])

    live_rows = LIVE * RPS
    r, c = iota((live_rows, ROWS), 0), iota((live_rows, ROWS), 1)
    q_pick = one_hot(c == (r & 3) * SLOTS + (r >> 4))
    spread = dot(q_pick, ext[0, 0:ROWS])
    r, c = iota((live_rows, FEAT), 0), iota((live_rows, FEAT), 1)
    qb[0:live_rows] = jnp.where((c >> 7) == ((r >> 2) & 3), spread, 0.0).astype(BF16)

    pl.semaphore_wait(barrier, len(near) + z)
    land_copy = pltpu.make_async_remote_copy(
        src_ref=land_src, dst_ref=land_dst, send_sem=land_sem.at[0], recv_sem=land_sem.at[1],
        device_id=x_peer, device_id_type=MESH)
    land_copy.start()
    for k in range(2 * NZ):
        w_push(k).start()
    lax.fori_loop(0, z, answer_below, 0)

    r, c = iota((live_rows, ROWS), 0), iota((live_rows, ROWS), 1)
    raw = dot_t(qb[0:live_rows], ext[1, 0:ROWS])
    sn[...] = jnp.where(((c & 31) == (r >> 4)) & ((c >> 5) <= (r & 3)), raw * SCALE, -jnp.inf)

    for cp in k_copies:
        cp.wait()
    for k in range(2 * NZ):
        w_copy(k).start()
    lane = iota((RPS, PAGE), 1)

    def cache_scores(i):
        page = jnp.minimum(table[0, i], LIVE_PAGES - 1)
        raw = dot_t(qb[i * RPS:(i + 1) * RPS], kbuf[page])
        sc[i * RPS:(i + 1) * RPS] = jnp.where(lane < lens[g * SLOTS + i], raw * SCALE, -jnp.inf)

    for i in range(LIVE):
        cache_scores(i)

    part = 240

    def soft(n, _):
        at = pl.ds(pl.multiple_of(n * part, part), part)
        a, b = sc[at], sn[at]
        top = jnp.max(jnp.maximum(a, b), axis=1, keepdims=True)
        ea, eb = jnp.exp(a - top), jnp.exp(b - top)
        inv = 1.0 / jnp.sum(ea + eb, axis=1, keepdims=True)
        pc[at] = (ea * inv).astype(BF16)
        pn[at] = (eb * inv).astype(BF16)
        return 0

    lax.fori_loop(0, live_rows // part, soft, 0)

    for cp in v_copies:
        cp.wait()
    c, r = iota((RPS, FEAT), 1), iota((RPS, FEAT), 0)
    diag = (c >> 7) == (r >> 2)
    on[...] = dot(pn[...], ext[2, 0:ROWS])

    for i in range(LIVE):
        at = pl.ds(i * RPS, RPS)
        page = jnp.minimum(table[0, i], LIVE_PAGES - 1)
        acc = on[at] + dot(pc[at], vbuf[page])
        ob[at] = jnp.where(diag, acc, 0.0).astype(BF16)

    r, c = iota((ROWS, live_rows), 0), iota((ROWS, live_rows), 1)
    slot = r & 31
    keep = ((r >> 5) == (c & 3)) & (slot == (c >> 4)) & (slot != mv_slot[0]) & (slot != mv_slot[1])
    attn[:, 0:FEAT] = dot(one_hot(keep), ob[0:live_rows]).astype(BF16)
    attn_copy = pltpu.make_async_remote_copy(
        src_ref=attn.at[:, pl.ds(0, FEAT)], dst_ref=attn.at[:, pl.ds(FEAT, FEAT)], send_sem=core_sem.at[0], recv_sem=core_sem.at[1],
        device_id=sibling, device_id_type=MESH)
    attn_copy.start()

    land_copy.wait_recv()
    for n in range(3):
        ext[n, ROWS:ROWS + 16] = land_dst[n]
    r, c = iota((32, 256), 0), iota((32, 256), 1)
    m, s = r >> 4, r & 3
    early = s < pick(m, mv_arr)
    mv_pick = one_hot((early & (c == s * SLOTS + pick(m, mv_row))) | (~early & (c == ROWS + m * 4 + s)))
    spread = dot(mv_pick, ext[0])
    r, c = iota((32, FEAT), 0), iota((32, FEAT), 1)
    qm = jnp.where((c >> 7) == ((r >> 2) & 3), spread, 0.0).astype(BF16)
    qb[live_rows:] = qm
    r, c = iota((32, 256), 0), iota((32, 256), 1)
    m, s = r >> 4, r & 3
    arr, row = pick(m, mv_arr), pick(m, mv_row)
    u_own, u_land = c >> 5, c & 3
    ok_own = (c < ROWS) & ((c & 31) == row) & (u_own < arr) & (u_own <= s)
    ok_land = (c >= ROWS) & (c < ROWS + 8) & (((c >> 2) & 1) == m) & (u_land >= arr) & (u_land <= s)
    sm = jnp.where(ok_own | ok_land, dot_t(qm, ext[1]) * SCALE, -jnp.inf)
    mv_page = [[jnp.minimum(table[j, mv_row[m]], LIVE_PAGES - 1) for j in range(MAXP)] for m in range(2)]
    for m in range(2):
        q_one = qb[live_rows + m * RPS:live_rows + (m + 1) * RPS]
        for j in range(MAXP):
            raw = dot_t(q_one, kbuf[mv_page[m][j]])
            scm[m * RPS:(m + 1) * RPS, j * PAGE:(j + 1) * PAGE] = jnp.where(
                lane + j * PAGE < lens[g * SLOTS + mv_row[m]], raw * SCALE, -jnp.inf)
    a = scm[...]
    top = jnp.maximum(jnp.max(a, axis=1, keepdims=True), jnp.max(sm, axis=1, keepdims=True))
    ea, eb = jnp.exp(a - top), jnp.exp(sm - top)
    inv = 1.0 / (jnp.sum(ea, axis=1, keepdims=True) + jnp.sum(eb, axis=1, keepdims=True))
    scm[...] = ea * inv
    om_new = dot((eb * inv).astype(BF16), ext[2])
    for m in range(2):
        acc = om_new[m * RPS:(m + 1) * RPS]
        for j in range(MAXP):
            acc = acc + dot(scm[m * RPS:(m + 1) * RPS, j * PAGE:(j + 1) * PAGE].astype(BF16), vbuf[mv_page[m][j]])
        ob[live_rows + m * RPS:live_rows + (m + 1) * RPS] = jnp.where(diag, acc, 0.0).astype(BF16)
    r, c = iota((16, 32), 0), iota((16, 32), 1)
    gather = one_hot(((c >> 4) == (r >> 2)) & ((c & 3) == (r & 3)))
    moved = dot(gather, ob[live_rows:])
    moved_src[...] = moved.astype(BF16)
    moved_copies = [pltpu.make_async_remote_copy(
        src_ref=moved_src, dst_ref=moved_dst.at[n], send_sem=moved_ssem.at[n], recv_sem=moved_rsem.at[n],
        device_id=peer, device_id_type=MESH) for n, peer in enumerate((x_peer, x_sibling, sibling))]
    for cp in moved_copies:
        cp.start()

    low = iota((64, HD), 1) < 64
    core0 = core == 0

    def project(k):
        w_copy(k).wait()
        w_push(k).wait_recv()
        res = dot(attn[...], wbuf[k])
        one, two = res[:, 0:HD], res[:, HD:2 * HD]
        left = jnp.where(low, two[0:64], pltpu.roll(two[64:ROWS], 64, 1))
        right = jnp.where(low, pltpu.roll(one[0:64], 64, 1), one[64:ROWS])
        return jnp.where(core0, one, two), jnp.where(core0, left, right)

    def y_copy(k):
        return pltpu.make_async_remote_copy(
            src_ref=y_src.at[k], dst_ref=y_dst.at[k], send_sem=y_ssem.at[k], recv_sem=y_rsem.at[k],
            device_id=y_peer, device_id_type=MESH)

    def z_copy(k, slot):
        return pltpu.make_async_remote_copy(
            src_ref=z_src.at[k], dst_ref=z_dst.at[slot], send_sem=z_ssem.at[k], recv_sem=z_rsem.at[slot],
            device_id=z_device(z_at(k)), device_id_type=MESH)

    def slot_at(k):
        return z - jnp.where(z > z_at(k), 1, 0)

    def send_home(k):
        y_copy(k).wait_recv()
        z_src[k] = (own[k] + y_dst[k].astype(F32)).astype(BF16)
        z_copy(k, slot_at(k)).start()

    attn_copy.wait_recv()
    for k in range(NZ):
        side, mid = project(k)
        y_src[k, 0:ROWS] = side.astype(BF16)
        y_src[k, ROWS:UNIT] = mid.astype(BF16)
        y_copy(k).start()
    for k in range(NZ):
        own[k, 0:ROWS], own[k, ROWS:UNIT] = project(NZ + k)

    for cp in moved_copies:
        cp.wait_recv()
    r = iota((16, FEAT), 0)
    m, s = (r >> 2) & 1, r & 3
    leaves = (r < 8) & (s < pick(m, mv_arr))
    lands = (r < 8) & (s >= pick(m, in_arr)) & (pick(m, in_slot) < LIVE)
    for n, mine in enumerate((moved, moved_dst[2].astype(F32))):
        attn_c[:, n * FEAT:(n + 1) * FEAT] = jnp.where(
            leaves, mine, jnp.where(lands, moved_dst[n].astype(F32), 0.0)).astype(BF16)

    def yc_copy(k, slot):
        return pltpu.make_async_remote_copy(
            src_ref=yc_src.at[k], dst_ref=yc_dst.at[slot], send_sem=yc_ssem.at[k], recv_sem=yc_rsem.at[slot],
            device_id=(g, (1 - yh) * 16 + z_at(k) * 2 + core), device_id_type=MESH)

    def zc_copy(k, slot):
        return pltpu.make_async_remote_copy(
            src_ref=zc_src.at[k], dst_ref=zc_dst.at[slot], send_sem=zc_ssem.at[k], recv_sem=zc_rsem.at[slot],
            device_id=z_device(z_at(k)), device_id_type=MESH)

    def project_c(k):
        res = dot(attn_c[...], wbuf[k])
        one, two = res[0:8, 0:HD], res[0:8, HD:2 * HD]
        return jnp.concatenate([jnp.where(core0, one, two), jnp.where(core0, two, one)], 0)

    @pl.when(z < NZ - 1)
    def _():
        pl.semaphore_wait(above_sem, NZ - 1 - z)

    send_home(0)
    for k in range(NZ):
        yc_src[k] = project_c(k).astype(BF16)
    for k in range(NZ):
        yc_copy(k, z).start()
    for k in range(NZ - 1):
        zc_src[k] = project_c(NZ + k).astype(BF16)
    for k in range(NZ - 1):
        zc_copy(k, slot_at(k)).start()
    total_c = project_c(2 * NZ - 1)
    for k in range(1, NZ - 1):
        send_home(k)
    y_copy(NZ - 1).wait_recv()
    total = own[NZ - 1] + y_dst[NZ - 1].astype(F32)
    for k in range(NZ - 1):
        z_copy(0, k).wait_recv()
        total = total + z_dst[k].astype(F32)
    for k in range(NZ - 1):
        zc_copy(0, k).wait_recv()
        total_c = total_c + zc_dst[k].astype(F32)
    for k in range(NZ):
        yc_copy(0, k).wait_recv()
        total_c = total_c + yc_dst[k].astype(F32)

    def columns(side, middle, first):
        turned = pltpu.roll(side, 64, 1)
        return jnp.where(core0, side, jnp.where(first, middle, turned)), jnp.where(core0, middle, turned)

    mid = total[ROWS:UNIT]
    one, two = columns(total[0:ROWS], jnp.concatenate([mid, pltpu.roll(mid, 64, 1)], 0), iota((ROWS, HD), 1) < 64)
    mid = total_c[8:16]
    one_c, two_c = columns(total_c[0:8], jnp.where(core0, mid, pltpu.roll(mid, 64, 1)), iota((8, HD), 1) < 64)
    rest = jnp.zeros((8, HD), F32)
    r, c = iota((ROWS, 16), 0), iota((ROWS, 16), 1)
    slot, step, m = r & 31, r >> 5, (c >> 2) & 1
    lands = (slot == LIVE + m) & (step >= pick(m, in_arr)) & (pick(m, in_slot) < LIVE)
    leaves = (slot == pick(m, mv_slot)) & (step < pick(m, mv_arr))
    place = one_hot((c < 8) & (step == (c & 3)) & (lands | leaves))
    one = one + dot(place, jnp.concatenate([one_c, rest], 0).astype(BF16))
    two = two + dot(place, jnp.concatenate([two_c, rest], 0).astype(BF16))
    out[:, 0:HD] = one.astype(BF16)
    out[:, HD:UNIT] = two[:, 0:64].astype(BF16)

    for cp in [land_copy, attn_copy] + moved_copies:
        cp.wait_send()
    for k in range(2 * NZ):
        w_push(k).wait_send()
    for k in range(NZ):
        y_copy(k).wait_send()
        yc_copy(k, 0).wait_send()
    for k in range(NZ - 1):
        z_copy(k, 0).wait_send()
        zc_copy(k, 0).wait_send()


def per_device(kv, qkv, w, table, lens, plan):
    vmem, sems = pltpu.VMEM, pltpu.SemaphoreType.DMA
    hbm = pl.BlockSpec(memory_space=pltpu.HBM)
    unit = (UNIT, HD)
    res = pl.pallas_call(
        kernel,
        out_shape=jax.ShapeDtypeStruct((ROWS, UNIT), BF16),
        in_specs=[hbm] * 6,
        out_specs=pl.BlockSpec(memory_space=pltpu.VMEM),
        scratch_shapes=[
            pltpu.SMEM((MAXP, SLOTS), jnp.int32), pltpu.SMEM(lens.shape, jnp.int32), pltpu.SMEM(plan.shape[::-1], jnp.int32),
            vmem((LIVE_PAGES, PAGE, FEAT), BF16), vmem((LIVE_PAGES, PAGE, FEAT), BF16), vmem((2 * NZ, 2 * FEAT, 2 * HD), BF16),
            vmem((3, 256, FEAT), BF16), vmem((3, 16, FEAT), BF16), vmem((3, 16, FEAT), BF16),
            vmem((16, FEAT), BF16), vmem((3, 16, FEAT), BF16),
            vmem((512, FEAT), BF16), vmem((LIVE * RPS, PAGE), F32), vmem((LIVE * RPS, ROWS), F32), vmem((32, MAXP * PAGE), F32),
            vmem((LIVE * RPS, PAGE), BF16), vmem((LIVE * RPS, ROWS), BF16), vmem((LIVE * RPS, FEAT), F32),
            vmem((512, FEAT), BF16), vmem((ROWS, 2 * FEAT), BF16), vmem((16, 2 * FEAT), BF16),
            vmem((NZ,) + unit, F32), vmem((NZ,) + unit, BF16), vmem((NZ,) + unit, BF16),
            vmem((NZ - 1,) + unit, BF16), vmem((NZ - 1,) + unit, BF16),
            vmem((NZ, 16, HD), BF16), vmem((NZ, 16, HD), BF16),
            vmem((NZ - 1, 16, HD), BF16), vmem((NZ - 1, 16, HD), BF16),
            sems((3,)), sems((CHUNKS,)), sems((CHUNKS,)), sems((2 * NZ,)), sems, sems((2,)), sems((3,)), sems((3,)), sems((2,)),
            sems((2 * NZ,)), sems((2 * NZ,)), sems((NZ,)), sems((NZ,)), sems((NZ - 1,)), sems((NZ - 1,)),
            sems((NZ,)), sems((NZ,)), sems((NZ - 1,)), sems((NZ - 1,)), pltpu.SemaphoreType.REGULAR,
        ],
        compiler_params=pltpu.CompilerParams(collective_id=0, has_side_effects=True, vmem_limit_bytes=60 << 20),
    )(kv, qkv.reshape(3, ROWS, FEAT), w, table.T, lens, plan.T)
    return res.reshape(STEPS, SLOTS, UNIT)


def solution(mesh):
    return jax.shard_map(
        per_device,
        mesh=mesh,
        in_specs=(P(None, "grp", None, "head"), P(None, None, "grp", "head"), P("head", None), P("grp", None), P(), P()),
        out_specs=P(None, "grp", "head"),
        check_vma=False,
    )
```

```python
import jax
import jax.numpy as jnp
from jax import lax
from jax.experimental import pallas as pl
from jax.experimental.pallas import tpu as pltpu
from jax.sharding import PartitionSpec as P

MESH = pl.DeviceIdType.MESH
HD = 128
HEADS = 3
FEAT = HEADS * HD
STEPS = 4
SLOTS = 32
LIVE = 30
LIVE_PAGES = 36
PAGE = 128
MAXP = 4
ROWS = STEPS * SLOTS
RPS = 16
CHUNKS = 1
NZ = 8
FIRST_Z = (0, 1)
Z_ORDER = [[t for t in FIRST_Z if t != n] + sorted((t for t in range(NZ) if t != n and t not in FIRST_Z),
                                                   key=lambda t: -min((t - n) % NZ, (n - t) % NZ)) for n in range(NZ)]
UNIT = 192
F32 = jnp.float32
BF16 = jnp.bfloat16
SCALE = HD ** -0.5


def iota(shape, dim):
    return lax.broadcasted_iota(jnp.int32, shape, dim)


def one_hot(cond):
    return jnp.where(cond, 1.0, 0.0).astype(BF16)


def dot(a, b):
    return jnp.dot(a, b, preferred_element_type=F32)


def dot_t(a, b):
    return lax.dot_general(a, b, (((1,), (1,)), ((), ())), preferred_element_type=F32)


def kernel(kv, qkv, w, table_in, lens_in, plan_in, out,
           table, lens, plan, kbuf, vbuf, wbuf, ext, land_src, land_dst, moved_src, moved_dst,
           qb, sc, sn, scm, pc, pn, on, ob, attn, attn_c,
           own, y_src, y_dst, z_src, z_dst, yc_src, yc_dst, zc_src, zc_dst,
           i_sem, k_sem, v_sem, w_sem, q_sem, land_sem, moved_ssem, moved_rsem, core_sem,
           wp_ssem, wp_rsem, y_ssem, y_rsem, z_ssem, z_rsem, yc_ssem, yc_rsem, zc_ssem, zc_rsem, above_sem):
    g = lax.axis_index("grp")
    h = lax.axis_index("head")
    yh, z, core = h // 16, lax.rem(h // 2, NZ), lax.rem(h, 2)
    sibling = (g, h + 1 - 2 * core)
    y_peer = (g, lax.rem(h + 16, 32))
    pair = lax.rem(g + 4, 8)
    x_peer = (pair, h)

    def z_device(t):
        return (g, yh * 16 + t * 2 + core)

    def z_at(k):
        if k == NZ - 1:
            return z
        t = Z_ORDER[0][k]
        for n in range(1, NZ):
            t = jnp.where(z == n, Z_ORDER[n][k], t)
        return t

    q_copy = pltpu.make_async_copy(qkv, ext.at[:, pl.ds(0, ROWS)], q_sem)
    q_copy.start()
    i_copies = [pltpu.make_async_copy(src, dst, i_sem.at[n])
                for n, (src, dst) in enumerate(((table_in, table), (lens_in, lens), (plan_in, plan)))]
    for cp in i_copies:
        cp.start()
    per = LIVE_PAGES // CHUNKS

    def page_copies(which, buf, sem):
        return [pltpu.make_async_copy(kv.at[which, pl.ds(n * per, per)], buf.at[pl.ds(n * per, per)], sem.at[n])
                for n in range(CHUNKS)]

    k_copies = page_copies(0, kbuf, k_sem)
    v_copies = page_copies(1, vbuf, v_sem)
    for cp in k_copies + v_copies:
        cp.start()

    barrier = pltpu.get_barrier_semaphore()
    x_sibling = (pair, h + 1 - 2 * core)
    near = (sibling, y_peer, x_peer, x_sibling)
    for peer in near:
        pl.semaphore_signal(barrier, inc=1, device_id=peer, device_id_type=MESH)

    def greet_above(t, _):
        pl.semaphore_signal(barrier, inc=1, device_id=z_device(t), device_id_type=MESH)
        return 0

    def answer_below(t, _):
        pl.semaphore_signal(above_sem, inc=1, device_id=z_device(t), device_id_type=MESH)
        return 0

    lax.fori_loop(z + 1, NZ, greet_above, 0)

    def w_columns(k, c):
        b = (1 - yh) if k < NZ else yh
        return w.at[:, pl.ds(pl.multiple_of((b * NZ + z_at(k % NZ)) * FEAT + c * HD, HD), 2 * HD)]

    def w_copy(k):
        return pltpu.make_async_copy(w_columns(k, core), wbuf.at[k, pl.ds(0, FEAT)], w_sem.at[k])

    def w_push(k):
        return pltpu.make_async_remote_copy(
            src_ref=w_columns(k, 1 - core), dst_ref=wbuf.at[k, pl.ds(FEAT, FEAT)], send_sem=wp_ssem.at[k], recv_sem=wp_rsem.at[k],
            device_id=sibling, device_id_type=MESH)

    q_copy.wait()
    r, c = iota((16, ROWS), 0), iota((16, ROWS), 1)
    land_pick = one_hot((r < 8) & (c == (r & 3) * SLOTS + LIVE + (r >> 2)))
    for n in range(3):
        land_src[n] = dot(land_pick, ext[n, 0:ROWS]).astype(BF16)
        ext[n, ROWS + 16:256] = jnp.zeros((112, FEAT), BF16)

    for cp in i_copies:
        cp.wait()
    mv_slot = [plan[0, g * 2 + m] for m in range(2)]
    mv_arr = [plan[1, g * 2 + m] for m in range(2)]
    in_slot = [plan[0, pair * 2 + m] for m in range(2)]
    in_arr = [plan[1, pair * 2 + m] for m in range(2)]
    mv_row = [jnp.minimum(s, LIVE - 1) for s in mv_slot]

    def pick(m, values):
        return jnp.where(m == 0, values[0], values[1])

    live_rows = LIVE * RPS
    r, c = iota((live_rows, ROWS), 0), iota((live_rows, ROWS), 1)
    q_pick = one_hot(c == (r & 3) * SLOTS + (r >> 4))
    spread = dot(q_pick, ext[0, 0:ROWS])
    r, c = iota((live_rows, FEAT), 0), iota((live_rows, FEAT), 1)
    qb[0:live_rows] = jnp.where((c >> 7) == ((r >> 2) & 3), spread, 0.0).astype(BF16)

    pl.semaphore_wait(barrier, len(near) + z)
    land_copy = pltpu.make_async_remote_copy(
        src_ref=land_src, dst_ref=land_dst, send_sem=land_sem.at[0], recv_sem=land_sem.at[1],
        device_id=x_peer, device_id_type=MESH)
    land_copy.start()
    for k in range(2 * NZ):
        w_push(k).start()
    lax.fori_loop(0, z, answer_below, 0)

    r, c = iota((live_rows, ROWS), 0), iota((live_rows, ROWS), 1)
    raw = dot_t(qb[0:live_rows], ext[1, 0:ROWS])
    sn[...] = jnp.where(((c & 31) == (r >> 4)) & ((c >> 5) <= (r & 3)), raw * SCALE, -jnp.inf)

    for cp in k_copies:
        cp.wait()
    for k in range(2 * NZ):
        w_copy(k).start()
    lane = iota((RPS, PAGE), 1)

    def cache_scores(i):
        page = jnp.minimum(table[0, i], LIVE_PAGES - 1)
        raw = dot_t(qb[i * RPS:(i + 1) * RPS], kbuf[page])
        sc[i * RPS:(i + 1) * RPS] = jnp.where(lane < lens[g * SLOTS + i], raw * SCALE, -jnp.inf)

    for i in range(LIVE):
        cache_scores(i)

    part = 240

    def soft(n, _):
        at = pl.ds(pl.multiple_of(n * part, part), part)
        a, b = sc[at], sn[at]
        top = jnp.max(jnp.maximum(a, b), axis=1, keepdims=True)
        ea, eb = jnp.exp(a - top), jnp.exp(b - top)
        inv = 1.0 / jnp.sum(ea + eb, axis=1, keepdims=True)
        pc[at] = (ea * inv).astype(BF16)
        pn[at] = (eb * inv).astype(BF16)
        return 0

    lax.fori_loop(0, live_rows // part, soft, 0)

    for cp in v_copies:
        cp.wait()
    c, r = iota((RPS, FEAT), 1), iota((RPS, FEAT), 0)
    diag = (c >> 7) == (r >> 2)
    on[...] = dot(pn[...], ext[2, 0:ROWS])

    for i in range(LIVE):
        at = pl.ds(i * RPS, RPS)
        page = jnp.minimum(table[0, i], LIVE_PAGES - 1)
        acc = on[at] + dot(pc[at], vbuf[page])
        ob[at] = jnp.where(diag, acc, 0.0).astype(BF16)

    r, c = iota((ROWS, live_rows), 0), iota((ROWS, live_rows), 1)
    slot = r & 31
    keep = ((r >> 5) == (c & 3)) & (slot == (c >> 4)) & (slot != mv_slot[0]) & (slot != mv_slot[1])
    attn[:, 0:FEAT] = dot(one_hot(keep), ob[0:live_rows]).astype(BF16)
    attn_copy = pltpu.make_async_remote_copy(
        src_ref=attn.at[:, pl.ds(0, FEAT)], dst_ref=attn.at[:, pl.ds(FEAT, FEAT)], send_sem=core_sem.at[0], recv_sem=core_sem.at[1],
        device_id=sibling, device_id_type=MESH)
    attn_copy.start()

    land_copy.wait_recv()
    for n in range(3):
        ext[n, ROWS:ROWS + 16] = land_dst[n]
    r, c = iota((32, 256), 0), iota((32, 256), 1)
    m, s = r >> 4, r & 3
    early = s < pick(m, mv_arr)
    mv_pick = one_hot((early & (c == s * SLOTS + pick(m, mv_row))) | (~early & (c == ROWS + m * 4 + s)))
    spread = dot(mv_pick, ext[0])
    r, c = iota((32, FEAT), 0), iota((32, FEAT), 1)
    qm = jnp.where((c >> 7) == ((r >> 2) & 3), spread, 0.0).astype(BF16)
    qb[live_rows:] = qm
    r, c = iota((32, 256), 0), iota((32, 256), 1)
    m, s = r >> 4, r & 3
    arr, row = pick(m, mv_arr), pick(m, mv_row)
    u_own, u_land = c >> 5, c & 3
    ok_own = (c < ROWS) & ((c & 31) == row) & (u_own < arr) & (u_own <= s)
    ok_land = (c >= ROWS) & (c < ROWS + 8) & (((c >> 2) & 1) == m) & (u_land >= arr) & (u_land <= s)
    sm = jnp.where(ok_own | ok_land, dot_t(qm, ext[1]) * SCALE, -jnp.inf)
    mv_page = [[jnp.minimum(table[j, mv_row[m]], LIVE_PAGES - 1) for j in range(MAXP)] for m in range(2)]
    for m in range(2):
        q_one = qb[live_rows + m * RPS:live_rows + (m + 1) * RPS]
        for j in range(MAXP):
            raw = dot_t(q_one, kbuf[mv_page[m][j]])
            scm[m * RPS:(m + 1) * RPS, j * PAGE:(j + 1) * PAGE] = jnp.where(
                lane + j * PAGE < lens[g * SLOTS + mv_row[m]], raw * SCALE, -jnp.inf)
    a = scm[...]
    top = jnp.maximum(jnp.max(a, axis=1, keepdims=True), jnp.max(sm, axis=1, keepdims=True))
    ea, eb = jnp.exp(a - top), jnp.exp(sm - top)
    inv = 1.0 / (jnp.sum(ea, axis=1, keepdims=True) + jnp.sum(eb, axis=1, keepdims=True))
    scm[...] = ea * inv
    om_new = dot((eb * inv).astype(BF16), ext[2])
    for m in range(2):
        acc = om_new[m * RPS:(m + 1) * RPS]
        for j in range(MAXP):
            acc = acc + dot(scm[m * RPS:(m + 1) * RPS, j * PAGE:(j + 1) * PAGE].astype(BF16), vbuf[mv_page[m][j]])
        ob[live_rows + m * RPS:live_rows + (m + 1) * RPS] = jnp.where(diag, acc, 0.0).astype(BF16)
    r, c = iota((16, 32), 0), iota((16, 32), 1)
    gather = one_hot(((c >> 4) == (r >> 2)) & ((c & 3) == (r & 3)))
    moved = dot(gather, ob[live_rows:])
    moved_src[...] = moved.astype(BF16)
    moved_copies = [pltpu.make_async_remote_copy(
        src_ref=moved_src, dst_ref=moved_dst.at[n], send_sem=moved_ssem.at[n], recv_sem=moved_rsem.at[n],
        device_id=peer, device_id_type=MESH) for n, peer in enumerate((x_peer, x_sibling, sibling))]
    for cp in moved_copies:
        cp.start()

    low = iota((64, HD), 1) < 64
    core0 = core == 0

    def project(k):
        w_copy(k).wait()
        w_push(k).wait_recv()
        res = dot(attn[...], wbuf[k])
        one, two = res[:, 0:HD], res[:, HD:2 * HD]
        left = jnp.where(low, two[0:64], pltpu.roll(two[64:ROWS], 64, 1))
        right = jnp.where(low, pltpu.roll(one[0:64], 64, 1), one[64:ROWS])
        return jnp.where(core0, one, two), jnp.where(core0, left, right)

    def y_copy(k):
        return pltpu.make_async_remote_copy(
            src_ref=y_src.at[k], dst_ref=y_dst.at[k], send_sem=y_ssem.at[k], recv_sem=y_rsem.at[k],
            device_id=y_peer, device_id_type=MESH)

    def z_copy(k, slot):
        return pltpu.make_async_remote_copy(
            src_ref=z_src.at[k], dst_ref=z_dst.at[slot], send_sem=z_ssem.at[k], recv_sem=z_rsem.at[slot],
            device_id=z_device(z_at(k)), device_id_type=MESH)

    def slot_at(k):
        return z - jnp.where(z > z_at(k), 1, 0)

    def send_home(k):
        y_copy(k).wait_recv()
        z_src[k] = (own[k] + y_dst[k].astype(F32)).astype(BF16)
        z_copy(k, slot_at(k)).start()

    attn_copy.wait_recv()
    for k in range(NZ):
        side, mid = project(k)
        y_src[k, 0:ROWS] = side.astype(BF16)
        y_src[k, ROWS:UNIT] = mid.astype(BF16)
        y_copy(k).start()
    for k in range(NZ):
        own[k, 0:ROWS], own[k, ROWS:UNIT] = project(NZ + k)

    for cp in moved_copies:
        cp.wait_recv()
    r = iota((16, FEAT), 0)
    m, s = (r >> 2) & 1, r & 3
    leaves = (r < 8) & (s < pick(m, mv_arr))
    lands = (r < 8) & (s >= pick(m, in_arr)) & (pick(m, in_slot) < LIVE)
    for n, mine in enumerate((moved, moved_dst[2].astype(F32))):
        attn_c[:, n * FEAT:(n + 1) * FEAT] = jnp.where(
            leaves, mine, jnp.where(lands, moved_dst[n].astype(F32), 0.0)).astype(BF16)

    def yc_copy(k, slot):
        return pltpu.make_async_remote_copy(
            src_ref=yc_src.at[k], dst_ref=yc_dst.at[slot], send_sem=yc_ssem.at[k], recv_sem=yc_rsem.at[slot],
            device_id=(g, (1 - yh) * 16 + z_at(k) * 2 + core), device_id_type=MESH)

    def zc_copy(k, slot):
        return pltpu.make_async_remote_copy(
            src_ref=zc_src.at[k], dst_ref=zc_dst.at[slot], send_sem=zc_ssem.at[k], recv_sem=zc_rsem.at[slot],
            device_id=z_device(z_at(k)), device_id_type=MESH)

    def project_c(k):
        res = dot(attn_c[...], wbuf[k])
        one, two = res[0:8, 0:HD], res[0:8, HD:2 * HD]
        return jnp.concatenate([jnp.where(core0, one, two), jnp.where(core0, two, one)], 0)

    @pl.when(z < NZ - 1)
    def _():
        pl.semaphore_wait(above_sem, NZ - 1 - z)

    send_home(0)
    for k in range(NZ):
        yc_src[k] = project_c(k).astype(BF16)
    for k in range(NZ):
        yc_copy(k, z).start()
    for k in range(NZ - 1):
        zc_src[k] = project_c(NZ + k).astype(BF16)
    for k in range(NZ - 1):
        zc_copy(k, slot_at(k)).start()
    total_c = project_c(2 * NZ - 1)
    for k in range(1, NZ - 1):
        send_home(k)
    for k in range(NZ - 1):
        zc_copy(0, k).wait_recv()
        total_c = total_c + zc_dst[k].astype(F32)
    for k in range(NZ):
        yc_copy(0, k).wait_recv()
        total_c = total_c + yc_dst[k].astype(F32)

    def columns(side, middle, first):
        turned = pltpu.roll(side, 64, 1)
        return jnp.where(core0, side, jnp.where(first, middle, turned)), jnp.where(core0, middle, turned)

    mid = total_c[8:16]
    one_c, two_c = columns(total_c[0:8], jnp.where(core0, mid, pltpu.roll(mid, 64, 1)), iota((8, HD), 1) < 64)
    rest = jnp.zeros((8, HD), F32)
    r, c = iota((ROWS, 16), 0), iota((ROWS, 16), 1)
    slot, step, m = r & 31, r >> 5, (c >> 2) & 1
    lands = (slot == LIVE + m) & (step >= pick(m, in_arr)) & (pick(m, in_slot) < LIVE)
    leaves = (slot == pick(m, mv_slot)) & (step < pick(m, mv_arr))
    place = one_hot((c < 8) & (step == (c & 3)) & (lands | leaves))
    add_one = dot(place, jnp.concatenate([one_c, rest], 0).astype(BF16))
    add_two = dot(place, jnp.concatenate([two_c, rest], 0).astype(BF16))
    y_copy(NZ - 1).wait_recv()
    total = own[NZ - 1] + y_dst[NZ - 1].astype(F32)
    for k in range(NZ - 1):
        z_copy(0, k).wait_recv()
        total = total + z_dst[k].astype(F32)
    mid = total[ROWS:UNIT]
    one, two = columns(total[0:ROWS], jnp.concatenate([mid, pltpu.roll(mid, 64, 1)], 0), iota((ROWS, HD), 1) < 64)
    one, two = one + add_one, two + add_two
    out[:, 0:HD] = one.astype(BF16)
    out[:, HD:UNIT] = two[:, 0:64].astype(BF16)

    for cp in [land_copy, attn_copy] + moved_copies:
        cp.wait_send()
    for k in range(2 * NZ):
        w_push(k).wait_send()
    for k in range(NZ):
        y_copy(k).wait_send()
        yc_copy(k, 0).wait_send()
    for k in range(NZ - 1):
        z_copy(k, 0).wait_send()
        zc_copy(k, 0).wait_send()


def per_device(kv, qkv, w, table, lens, plan):
    vmem, sems = pltpu.VMEM, pltpu.SemaphoreType.DMA
    hbm = pl.BlockSpec(memory_space=pltpu.HBM)
    unit = (UNIT, HD)
    res = pl.pallas_call(
        kernel,
        out_shape=jax.ShapeDtypeStruct((ROWS, UNIT), BF16),
        in_specs=[hbm] * 6,
        out_specs=pl.BlockSpec(memory_space=pltpu.VMEM),
        scratch_shapes=[
            pltpu.SMEM((MAXP, SLOTS), jnp.int32), pltpu.SMEM(lens.shape, jnp.int32), pltpu.SMEM(plan.shape[::-1], jnp.int32),
            vmem((LIVE_PAGES, PAGE, FEAT), BF16), vmem((LIVE_PAGES, PAGE, FEAT), BF16), vmem((2 * NZ, 2 * FEAT, 2 * HD), BF16),
            vmem((3, 256, FEAT), BF16), vmem((3, 16, FEAT), BF16), vmem((3, 16, FEAT), BF16),
            vmem((16, FEAT), BF16), vmem((3, 16, FEAT), BF16),
            vmem((512, FEAT), BF16), vmem((LIVE * RPS, PAGE), F32), vmem((LIVE * RPS, ROWS), F32), vmem((32, MAXP * PAGE), F32),
            vmem((LIVE * RPS, PAGE), BF16), vmem((LIVE * RPS, ROWS), BF16), vmem((LIVE * RPS, FEAT), F32),
            vmem((512, FEAT), BF16), vmem((ROWS, 2 * FEAT), BF16), vmem((16, 2 * FEAT), BF16),
            vmem((NZ,) + unit, F32), vmem((NZ,) + unit, BF16), vmem((NZ,) + unit, BF16),
            vmem((NZ - 1,) + unit, BF16), vmem((NZ - 1,) + unit, BF16),
            vmem((NZ, 16, HD), BF16), vmem((NZ, 16, HD), BF16),
            vmem((NZ - 1, 16, HD), BF16), vmem((NZ - 1, 16, HD), BF16),
            sems((3,)), sems((CHUNKS,)), sems((CHUNKS,)), sems((2 * NZ,)), sems, sems((2,)), sems((3,)), sems((3,)), sems((2,)),
            sems((2 * NZ,)), sems((2 * NZ,)), sems((NZ,)), sems((NZ,)), sems((NZ - 1,)), sems((NZ - 1,)),
            sems((NZ,)), sems((NZ,)), sems((NZ - 1,)), sems((NZ - 1,)), pltpu.SemaphoreType.REGULAR,
        ],
        compiler_params=pltpu.CompilerParams(collective_id=0, has_side_effects=True, vmem_limit_bytes=60 << 20),
    )(kv, qkv.reshape(3, ROWS, FEAT), w, table.T, lens, plan.T)
    return res.reshape(STEPS, SLOTS, UNIT)


def solution(mesh):
    return jax.shard_map(
        per_device,
        mesh=mesh,
        in_specs=(P(None, "grp", None, "head"), P(None, None, "grp", "head"), P("head", None), P("grp", None), P(), P()),
        out_specs=P(None, "grp", "head"),
        check_vma=False,
    )
```
